32 devices in a mesh: node: 8 (over z, x), local: 4 (over y, core).
Axes of the slice: x: 2, y: 2, z: 4, core: 2. Of those that a mesh axis runs over, the one named last changes fastest.
Arguments:
- layer_input: bfloat16 [1024, 3584], P('node', 'local'), may hold values from -6 to 6
- output_grad: bfloat16 [1024, 3584], P('node', 'local'), may hold values from -6 to 6
- gate_weight: bfloat16 [8, 3584, 1024], P('node', None, 'local'), may hold values from -0.09375 to 0.09375
- up_weight: bfloat16 [8, 3584, 1024], P('node', None, 'local'), may hold values from -0.09375 to 0.09375
- down_weight: bfloat16 [8, 1024, 3584], P('node', 'local'), may hold values from -0.1875 to 0.1875
- route_offset: int32 [1024, 2], P('node'), may hold values from 0 to 3, all different within a row; in each aligned block of 128 rows (0 to 127, 128 to 255, ...) at most 80 rows name the same one
- gate_fixed: int32 [1024, 2], P('node'), may hold values from 4096 to 65535
Outputs:
- input_grad: bfloat16 [1024, 3584], P('node', 'local')
- gate_grad: float32 [1024, 2], P('node')
The draws below stay inside these ranges and needn't reach their ends.
Inputs may be any that keep to these rules, and one draw needn't show every extreme that they name: `route_offset`: each token names 2 different offsets. Among the 128 tokens of one node no offset is named more than 80 times, and in some node one offset is named exactly 80 times.
All inputs are finite; a program needn't handle non-finite values.
Results may differ from the reference program's by a relative error of at most 0.0049.
Values may be sent and summed in bfloat16 or wider, within the bound.
A program may use at most 64 MiB of HBM per device.

```python
import math
import jax
import jax.numpy as jnp
import numpy as np
from jax import lax

D = 3584
HID = 1024
GROUP = 4
TOPK = 2
NODE_TOK = 128
CAPACITY = 80
EXPERTS = 8
TOKENS = 1024
N_NODE = 8


def with_ends(entries, own_key, least, high):
    place = [jax.random.randint(jax.random.fold_in(own_key, axis), (), 0, length) for axis, length in enumerate(entries.shape)]
    widest = entries.shape.index(max(entries.shape))
    beside = place[:widest] + [(place[widest] + 1) % entries.shape[widest]] + place[widest + 1:]
    return entries.at[tuple(place)].set(least).at[tuple(beside)].set(high)


def shard_levels(key, shape, shards, low, top_value):
    def one(dim, shards_of):
        draws = jax.random.uniform(jax.random.fold_in(jax.random.fold_in(key, 6), dim), (shards_of,), jnp.float32, low / len(shards), top_value / len(shards))
        return jnp.repeat(jnp.exp(draws), shape[dim] // shards_of).reshape((-1,) + (1,) * (len(shape) - dim - 1))

    gain = one(*shards[0])
    for cut in shards[1:]:
        gain = gain * one(*cut)
    return gain


def routed_block(rng, own, number, rows, count, top, bound, slope):
    sequence = jax.random.permutation(rng, count)
    packed, ordinary = load_shares(count, rows * top, bound, slope, True), load_shares(count, rows * top, bound, slope, False)
    places = jnp.arange(count)

    def named(sizes, turn):
        used = int((sizes > 0).sum())
        fixed = max(1, used // 4)
        moved = fixed + (places - fixed + turn * (used - fixed)) % max(1, count - fixed)
        return jnp.zeros((count,), jnp.int32).at[sequence[jnp.where(places < fixed, places, moved)]].set(jnp.asarray(sizes, jnp.int32))

    sizes = jnp.where(number % 4 == 0, named(packed, number // 4), named(ordinary, number - number // 4 - 1))
    mixed = jax.random.permutation(jax.random.fold_in(own, 3), count)
    donor, taker = mixed[0:count // 2 * 2:2], mixed[1:count // 2 * 2:2]
    margin = jnp.minimum(sizes[donor] - 1, bound - sizes[taker]) // 2
    margin = jnp.where((donor == sequence[0]) | (taker == sequence[0]) | (sizes[taker] == 0), 0, jnp.maximum(margin, 0))
    moved = jax.random.randint(jax.random.fold_in(own, 4), (count // 2,), 0, 1 << 20) % (margin + 1)
    sizes = sizes.at[donor].add(-moved).at[taker].add(moved)
    items = jnp.searchsorted(jnp.cumsum(sizes), jnp.arange(rows * top), side="right").astype(jnp.int32)
    table = items.reshape(top, rows).T
    table = table[jax.random.permutation(jax.random.fold_in(own, 1), rows)]
    turn = jax.random.randint(jax.random.fold_in(own, 2), (rows, 1), 0, top)
    return jnp.take_along_axis(table, (jnp.arange(top)[None, :] + turn) % top, axis=1)


def load_shares(number_of, total, limit, slope, full):
    loads = [(1 << 20) // math.isqrt(standing ** slope) + 1 for standing in range(1, number_of + 1)]
    largest = limit if full else min(limit, max(-(-total // number_of), total * loads[0] // sum(loads)))
    least = 1 if total - largest >= number_of - 1 else 0
    holding, spare = [largest] + [least] * (number_of - 1), total - largest - least * (number_of - 1)
    while spare > 0:
        free = [i for i in range(1, number_of) if holding[i] < largest] or [i for i in range(1, number_of) if holding[i] < limit]
        whole, left = sum([loads[i] for i in free]), spare
        for i in free:
            more = min(limit - holding[i], max(1, left * loads[i] // whole), spare)
            holding[i] = holding[i] + more
            spare = spare - more
    return np.array(holding)


def noise(rng, dims, scale, bound, cuts=(), held_as=jnp.bfloat16):
    values = jax.random.normal(rng, dims, jnp.float32) * scale
    if len(cuts) > 0:
        values = shard_levels(rng, dims, cuts, -0.22, 0.18) * values
    return jnp.clip(values, min=-bound, max=bound).astype(held_as)


def setup_inputs(seed: int = 0) -> dict:
    arg_keys = jax.random.split(jax.random.key(seed), 8)
    layer_input = noise(arg_keys[0], (TOKENS, D), 1.0, 6.0, ((0, 8), (1, 4)))
    output_grad = noise(arg_keys[1], (TOKENS, D), 1.0, 6.0, ((0, 8), (1, 4)))
    gate_weight = noise(arg_keys[2], (EXPERTS, D, HID), D ** -0.5, 0.09375, ((0, 8), (2, 4)))
    up_weight = noise(arg_keys[3], (EXPERTS, D, HID), D ** -0.5, 0.09375, ((0, 8), (2, 4)))
    down_weight = noise(arg_keys[4], (EXPERTS, HID, D), HID ** -0.5, 0.1875, ((0, 8), (1, 4)))
    route_offset_keys = jax.random.split(jax.random.fold_in(arg_keys[5], 1), TOKENS // NODE_TOK)
    route_offset_turns = jax.random.permutation(jax.random.fold_in(arg_keys[5], 3), TOKENS // NODE_TOK)
    route_offset = jax.vmap(lambda own, number: routed_block(jax.random.fold_in(arg_keys[5], 2), own, number, NODE_TOK, GROUP, TOPK, CAPACITY, 2))(route_offset_keys, route_offset_turns).reshape((TOKENS, TOPK))
    gate_fixed = with_ends(jax.random.randint(arg_keys[6], (TOKENS, TOPK), 4096, 65536), jax.random.fold_in(arg_keys[6], 1), 4096, 65535).astype(jnp.int32)
    return dict(layer_input=layer_input, output_grad=output_grad, gate_weight=gate_weight, up_weight=up_weight, down_weight=down_weight, route_offset=route_offset, gate_fixed=gate_fixed)


def packer(chosen, capacity):
    ranks = jnp.cumsum(chosen.astype(jnp.int32)) - 1
    slots = jnp.arange(capacity, dtype=jnp.int32)
    return ((ranks[None, :] == slots[:, None]) & chosen[None, :]).astype(jnp.bfloat16)


def expert_backward(rows_in, rows_grad, gate_cols, up_cols, down_rows):
    gate_pre = jnp.dot(rows_in, gate_cols, preferred_element_type=jnp.float32)
    up_pre = jnp.dot(rows_in, up_cols, preferred_element_type=jnp.float32)
    hidden_grad = lax.dot_general(rows_grad, down_rows, (((1,), (1,)), ((), ())), preferred_element_type=jnp.float32)
    sigmoid = jax.nn.sigmoid(gate_pre)
    swish = gate_pre * sigmoid
    gate_part = jnp.sum(swish * up_pre * hidden_grad, axis=1)
    up_grad = (hidden_grad * swish).astype(jnp.bfloat16)
    pre_grad = (hidden_grad * up_pre * sigmoid * (1.0 + gate_pre * (1.0 - sigmoid))).astype(jnp.bfloat16)
    back = lax.dot_general(pre_grad, gate_cols, (((1,), (1,)), ((), ())), preferred_element_type=jnp.float32)
    back = back + lax.dot_general(up_grad, up_cols, (((1,), (1,)), ((), ())), preferred_element_type=jnp.float32)
    return back, gate_part


def reference(layer_input, output_grad, gate_weight, up_weight, down_weight, route_offset, gate_fixed):
    gates = gate_fixed.astype(jnp.float32) / 65536.0

    def visit(carry, expert):
        input_acc, gate_acc = carry
        gate_cols = lax.dynamic_index_in_dim(gate_weight, expert, 0, keepdims=False)
        up_cols = lax.dynamic_index_in_dim(up_weight, expert, 0, keepdims=False)
        down_rows = lax.dynamic_index_in_dim(down_weight, expert, 0, keepdims=False)
        for offset in range(GROUP):
            source = (expert - offset) % N_NODE
            start = (source * NODE_TOK).astype(jnp.int32)
            rows_in = lax.dynamic_slice_in_dim(layer_input, start, NODE_TOK, 0)
            rows_grad = lax.dynamic_slice_in_dim(output_grad, start, NODE_TOK, 0)
            routes = lax.dynamic_slice_in_dim(route_offset, start, NODE_TOK, 0)
            gate_rows = lax.dynamic_slice_in_dim(gates, start, NODE_TOK, 0)
            hits = routes == offset
            chosen = jnp.any(hits, axis=1)
            weight = jnp.sum(jnp.where(hits, gate_rows, jnp.zeros_like(gate_rows)), axis=1)
            table = packer(chosen, CAPACITY)
            packed_in = jnp.dot(table, rows_in, preferred_element_type=jnp.float32).astype(jnp.bfloat16)
            packed_grad = jnp.dot(table, rows_grad, preferred_element_type=jnp.float32).astype(jnp.bfloat16)
            back, gate_part = expert_backward(packed_in, packed_grad, gate_cols, up_cols, down_rows)
            spread = table.astype(jnp.float32)
            rows_back = lax.dot_general(spread, back, (((0,), (0,)), ((), ())), precision=lax.Precision.HIGHEST)
            gate_back = lax.dot_general(spread, gate_part, (((0,), (0,)), ((), ())), precision=lax.Precision.HIGHEST)
            old_rows = lax.dynamic_slice_in_dim(input_acc, start, NODE_TOK, 0)
            input_acc = lax.dynamic_update_slice_in_dim(input_acc, old_rows + weight[:, None] * rows_back, start, 0)
            old_gate = lax.dynamic_slice_in_dim(gate_acc, start, NODE_TOK, 0)
            added = jnp.where(hits, gate_back[:, None], jnp.zeros_like(old_gate))
            gate_acc = lax.dynamic_update_slice_in_dim(gate_acc, old_gate + added, start, 0)
        return (input_acc, gate_acc), None

    start_acc = (jnp.zeros(layer_input.shape, jnp.float32), jnp.zeros(gate_fixed.shape, jnp.float32))
    final, unused = lax.scan(visit, start_acc, jnp.arange(N_NODE, dtype=jnp.int32))
    return final[0].astype(jnp.bfloat16), final[1]
```

```python
import functools

import jax
import jax.numpy as jnp
from jax import lax
from jax.experimental import pallas as pl
from jax.experimental.pallas import tpu as pltpu
from jax.sharding import PartitionSpec as P

GROUP = 4
CAPACITY = 80
LANES = 128
MESH = pl.DeviceIdType.MESH
NT = (((1,), (1,)), ((), ()))
TN = (((0,), (0,)), ((), ()))


def dot(a, b, dims=None):
    if dims is None:
        return jnp.dot(a, b, preferred_element_type=jnp.float32)
    return lax.dot_general(a, b, dims, preferred_element_type=jnp.float32)


def lane_index(rows):
    return lax.broadcasted_iota(jnp.int32, (rows, LANES), 1)


def split_gate(value):
    high = value.astype(jnp.bfloat16).astype(jnp.float32)
    low = value - high
    return jnp.where(lane_index(value.shape[0]) < LANES // 2, high, low).astype(jnp.bfloat16)


def join_gate(parts):
    lanes = lane_index(parts.shape[0])
    keep = (lanes == 0) | (lanes == LANES // 2)
    return jnp.sum(jnp.where(keep, parts.astype(jnp.float32), 0.0), axis=1, keepdims=True)


def kernel(
    nodes, locals_,
    x_ref, g_ref, gate_hbm, up_hbm, down_hbm, route_ref, fixed_ref,
    out_ref, ggrad_ref,
    gw, uw, dw, table, packed, got, out_a, in_a, own, own_gate, out_b, in_b, mine, out_h, in_h,
    wsem, ns, nr, hs, hr, ls, lr, sa, ra, sb, rb, sm, rm,
):
    tokens, feat = x_ref.shape
    wide = out_h.shape[2]
    gate_lanes = pl.ds(wide - LANES, LANES)
    his = locals_ // 2
    node, me = lax.axis_index("node"), lax.axis_index("local")
    hi, lo = me // 2, me % 2
    mate = hi * 2 + (1 - lo)

    def ahead(steps):
        return (lax.rem(node + steps + nodes, nodes), me)

    def beside(index):
        return (node, index)

    def turned(d):
        return lax.rem(hi + d, his)

    weights = [
        pltpu.make_async_copy(source.at[0], dest, wsem.at[i])
        for i, (source, dest) in enumerate(((gate_hbm, gw), (up_hbm, uw), (down_hbm, dw)))
    ]
    for copy in weights:
        copy.start()

    barrier = pltpu.get_barrier_semaphore()
    friends = [ahead(s) for o in range(1, GROUP) for s in (o, -o)]
    friends += [beside(turned(d) * 2 + lo) for d in range(1, his)]
    friends += [beside(mate)]
    for friend in friends:
        pl.semaphore_signal(barrier, inc=1, device_id=friend, device_id_type=MESH)

    def remote(source, dest, send, recv, device):
        return pltpu.make_async_remote_copy(
            src_ref=source, dst_ref=dest, send_sem=send, recv_sem=recv,
            device_id=device, device_id_type=MESH,
        )

    def to_node(o, k):
        return remote(packed.at[o, k], got.at[o, me, k], ns.at[o, k], nr.at[o, k], ahead(o))

    def to_hi(o, k, d):
        return remote(
            got.at[o, me, k], got.at[o, me, k], hs.at[o, k, d], hr.at[o, k, hi],
            beside(turned(d) * 2 + lo),
        )

    def from_hi(o, k, d):
        h = turned(d)
        slot = got.at[o, h * 2 + lo, k]
        return remote(slot, slot, hs.at[o, k, d], hr.at[o, k, h], beside(h * 2 + lo))

    def to_mate(o, k, h):
        slot = got.at[o, h * 2 + lo, k]
        return remote(slot, slot, ls.at[o, k, h], lr.at[o, k, h], beside(mate))

    def from_mate(o, k, h):
        slot = got.at[o, h * 2 + 1 - lo, k]
        return remote(slot, slot, ls.at[o, k, h], lr.at[o, k, h], beside(mate))

    def sum_mate(o):
        return remote(out_a.at[o], in_a.at[o], sa.at[o], ra.at[o], beside(mate))

    def sum_hi(o, d):
        h = turned(d)
        return remote(out_b.at[o, h], in_b.at[o, hi], sb.at[o, h], rb.at[o, hi], beside(h * 2 + lo))

    def sum_from_hi(o, d):
        h = turned(d)
        return remote(out_b.at[o, h], in_b.at[o, h], sb.at[o, h], rb.at[o, h], beside(h * 2 + lo))

    def to_home(o):
        return remote(out_h.at[o], in_h.at[o], sm.at[o], rm.at[o], ahead(-o))

    route = route_ref[...]
    lanes = lane_index(tokens)
    chosen = ((route[:, 0:1] == lanes) | (route[:, 1:2] == lanes)).astype(jnp.float32)
    row = lax.broadcasted_iota(jnp.int32, (tokens, tokens), 0)
    column = lax.broadcasted_iota(jnp.int32, (tokens, tokens), 1)
    below = (column <= row).astype(jnp.float32).astype(jnp.bfloat16)
    ranks = dot(below, chosen.astype(jnp.bfloat16))
    slots = lax.broadcasted_iota(jnp.int32, (tokens, CAPACITY), 1).astype(jnp.float32) + 1.0
    tables = []
    for o in range(GROUP):
        here = (ranks[:, o:o + 1] == slots) & (chosen[:, o:o + 1] > 0.5)
        tables.append(here.astype(jnp.float32).astype(jnp.bfloat16))
        table[o] = tables[o]

    def pack(o, k):
        source = x_ref if k == 0 else g_ref
        return dot(tables[o], source[...], TN).astype(jnp.bfloat16)

    for k in range(2):
        got[0, me, k] = pack(0, k)
    pl.semaphore_wait(barrier, len(friends))
    for k in range(2):
        for d in range(1, his):
            to_hi(0, k, d).start()
    for o in range(1, GROUP):
        for k in range(2):
            packed[o, k] = pack(o, k)
            to_node(o, k).start()
    for k in range(2):
        to_mate(0, k, hi).start()
    for copy in weights:
        copy.wait()

    def spread(o):
        for k in range(2):
            to_node(o, k).wait_recv()
            for d in range(1, his):
                to_hi(o, k, d).start()
            to_mate(o, k, hi).start()

    def pass_on(o):
        for k in range(2):
            for d in range(1, his):
                from_hi(o, k, d).wait_recv()
                to_mate(o, k, turned(d)).start()

    def compute(o):
        for k in range(2):
            for h in range(his):
                from_mate(o, k, h).wait_recv()
        a = b = v = None
        for l in range(locals_):
            rows = pl.ds(l * feat, feat)
            x, g = got[o, l, 0], got[o, l, 1]
            pa, pb, pv = dot(x, gw[rows, :]), dot(x, uw[rows, :]), dot(g, dw[:, rows], NT)
            a, b, v = (pa, pb, pv) if a is None else (a + pa, b + pb, v + pv)
        s = 1.0 / (1.0 + jnp.exp(-a))
        swish = a * s
        part = split_gate(jnp.sum(swish * b * v, axis=1, keepdims=True))
        u = (v * swish).astype(jnp.bfloat16)
        w = (v * b * s * (1.0 + a * (1.0 - s))).astype(jnp.bfloat16)

        def back(l):
            rows = pl.ds(pl.multiple_of(l * feat, 64), feat)
            return dot(w, gw[rows, :], NT) + dot(u, uw[rows, :], NT)

        for h in range(his):
            out_a[o, h, :, pl.ds(0, feat)] = back(h * 2 + 1 - lo).astype(jnp.bfloat16)
            out_a[o, h, :, gate_lanes] = part
        sum_mate(o).start()
        own_gate[...] = part
        for h in range(his):
            own[h] = back(h * 2 + lo)

    def add_mate(o):
        sum_mate(o).wait_recv()
        gate = split_gate(join_gate(own_gate[...]) + join_gate(in_a[o, 0, :, gate_lanes]))
        for d in range(1, his):
            h = turned(d)
            total = own[h] + in_a[o, h, :, pl.ds(0, feat)].astype(jnp.float32)
            out_b[o, h, :, pl.ds(0, feat)] = total.astype(jnp.bfloat16)
            out_b[o, h, :, gate_lanes] = gate
            sum_hi(o, d).start()
        mine[o] = own[hi] + in_a[o, hi, :, pl.ds(0, feat)].astype(jnp.float32)
        in_b[o, hi, :, gate_lanes] = gate

    def add_hi(o):
        total = mine[o]
        for d in range(1, his):
            sum_from_hi(o, d).wait_recv()
            total = total + in_b[o, turned(d), :, pl.ds(0, feat)].astype(jnp.float32)
        gate = join_gate(in_b[o, 0, :, gate_lanes])
        for h in range(1, his):
            gate = gate + join_gate(in_b[o, h, :, gate_lanes])
        out_h[o, :, pl.ds(0, feat)] = total.astype(jnp.bfloat16)
        out_h[o, :, gate_lanes] = split_gate(gate)

        @pl.when(o > 0)
        def _():
            to_home(o).start()

    def step(i, carry):
        @pl.when(i + 1 < GROUP)
        def _():
            spread(i + 1)

        @pl.when(i < GROUP)
        def _():
            pass_on(i)

        @pl.when((i >= 1) & (i <= GROUP))
        def _():
            add_mate(i - 1)

        @pl.when(i >= 2)
        def _():
            add_hi(i - 2)

        @pl.when(i < GROUP)
        def _():
            compute(i)

        return carry

    lax.fori_loop(0, GROUP + 2, step, 0)

    gates = fixed_ref[...].astype(jnp.float32) / 65536.0
    total = jnp.zeros((tokens, feat), jnp.float32)
    gate_total = jnp.zeros(gates.shape, jnp.float32)
    for o in range(GROUP):
        if o > 0:
            to_home(o).wait_recv()
        home = out_h if o == 0 else in_h
        hits = route == o
        weight = jnp.sum(jnp.where(hits, gates, 0.0), axis=1, keepdims=True)
        total = total + weight * dot(table[o], home[o, :, pl.ds(0, feat)])
        back_gate = join_gate(dot(table[o], home[o, :, gate_lanes]))
        gate_total = gate_total + jnp.where(hits, back_gate, 0.0)
    out_ref[...] = total.astype(jnp.bfloat16)
    ggrad_ref[...] = gate_total

    def finish(o, carry):
        for k in range(2):
            for d in range(1, his):
                to_hi(o, k, d).wait_send()
            for h in range(his):
                to_mate(o, k, h).wait_send()
        sum_mate(o).wait_send()
        for d in range(1, his):
            sum_hi(o, d).wait_send()

        @pl.when(o > 0)
        def _():
            for k in range(2):
                to_node(o, k).wait_send()
            to_home(o).wait_send()

        return carry

    lax.fori_loop(0, GROUP, finish, 0)


def body(nodes, locals_, layer_input, output_grad, gate_weight, up_weight, down_weight, route, fixed):
    tokens, feat = layer_input.shape
    width, hidden = gate_weight.shape[1:]
    his = locals_ // 2
    wide = -(-feat // LANES) * LANES + LANES
    bf16, f32 = jnp.bfloat16, jnp.float32
    vmem, dma = pltpu.VMEM, pltpu.SemaphoreType.DMA
    scratch = [
        vmem((width, hidden), bf16),
        vmem((width, hidden), bf16),
        vmem((hidden, width), bf16),
        vmem((GROUP, tokens, CAPACITY), bf16),
        vmem((GROUP, 2, CAPACITY, feat), bf16),
        vmem((GROUP, locals_, 2, CAPACITY, feat), bf16),
        vmem((GROUP, his, CAPACITY, wide), bf16),
        vmem((GROUP, his, CAPACITY, wide), bf16),
        vmem((his, CAPACITY, feat), f32),
        vmem((CAPACITY, LANES), bf16),
        vmem((GROUP, his, CAPACITY, wide), bf16),
        vmem((GROUP, his, CAPACITY, wide), bf16),
        vmem((GROUP, CAPACITY, feat), f32),
        vmem((GROUP, CAPACITY, wide), bf16),
        vmem((GROUP, CAPACITY, wide), bf16),
        dma((3,)),
        dma((GROUP, 2)),
        dma((GROUP, 2)),
        dma((GROUP, 2, his)),
        dma((GROUP, 2, his)),
        dma((GROUP, 2, his)),
        dma((GROUP, 2, his)),
        dma((GROUP,)),
        dma((GROUP,)),
        dma((GROUP, his)),
        dma((GROUP, his)),
        dma((GROUP,)),
        dma((GROUP,)),
    ]
    in_vmem, anywhere = pl.BlockSpec(memory_space=pltpu.VMEM), pl.BlockSpec(memory_space=pl.ANY)
    routed = GROUP * CAPACITY
    return pl.pallas_call(
        functools.partial(kernel, nodes, locals_),
        out_shape=(
            jax.ShapeDtypeStruct((tokens, feat), bf16),
            jax.ShapeDtypeStruct(fixed.shape, f32),
        ),
        in_specs=[in_vmem, in_vmem, anywhere, anywhere, anywhere, in_vmem, in_vmem],
        out_specs=(in_vmem, in_vmem),
        scratch_shapes=scratch,
        compiler_params=pltpu.CompilerParams(
            collective_id=0, has_side_effects=True, vmem_limit_bytes=48 * 1024 * 1024
        ),
        cost_estimate=pl.CostEstimate(
            flops=10 * routed * width * hidden,
            bytes_accessed=6 * width * hidden + 6 * tokens * feat,
            transcendentals=routed * hidden,
        ),
    )(layer_input, output_grad, gate_weight, up_weight, down_weight, route, fixed)


def solution(mesh):
    in_specs = (
        P("node", "local"),
        P("node", "local"),
        P("node", None, "local"),
        P("node", None, "local"),
        P("node", "local", None),
        P("node", None),
        P("node", None),
    )
    out_specs = (P("node", "local"), P("node", None))
    run = functools.partial(body, mesh.shape["node"], mesh.shape["local"])
    return jax.shard_map(run, mesh=mesh, in_specs=in_specs, out_specs=out_specs, check_vma=False)
```

```python
import functools

import jax
import jax.numpy as jnp
from jax import lax
from jax.experimental import pallas as pl
from jax.experimental.pallas import tpu as pltpu
from jax.sharding import PartitionSpec as P

GROUP = 4
CAPACITY = 80
LANES = 128
MESH = pl.DeviceIdType.MESH
NT = (((1,), (1,)), ((), ()))
TN = (((0,), (0,)), ((), ()))


def dot(a, b, dims=None):
    if dims is None:
        return jnp.dot(a, b, preferred_element_type=jnp.float32)
    return lax.dot_general(a, b, dims, preferred_element_type=jnp.float32)


def split_gate(value):
    high = value.astype(jnp.bfloat16).astype(jnp.float32)
    return jnp.concatenate((high, value - high), axis=0).astype(jnp.bfloat16)


def join_gate(parts):
    parts = parts.astype(jnp.float32)
    return parts[0:8] + parts[8:16]


def lay_down(column):
    wide = jnp.broadcast_to(column, (CAPACITY, LANES))
    rest = jnp.zeros((LANES - CAPACITY, LANES), jnp.float32)
    return jnp.concatenate((wide, rest), axis=0).T[0:8]


def stand_up(row):
    return jnp.broadcast_to(row, (LANES, row.shape[1])).T


def kernel(
    nodes, locals_,
    x_hbm, g_hbm, gate_hbm, up_hbm, down_hbm, route_hbm, fixed_hbm,
    out_ref, ggrad_ref,
    x_ref, g_ref, gw, uw, dw, route_ref, fixed_ref,
    table, packed, got, out_a, in_a, out_b, in_b, mine, out_h, in_h,
    gate_out_a, gate_in_a, gate_out_b, gate_in_b, gate_out_h, gate_in_h,
    wsem, ns, nr, hs, hr, ls, lr, sa, ra, sb, rb, sm, rm, sga, rga, sgb, rgb, sgm, rgm,
):
    tokens, feat = x_ref.shape
    his = locals_ // 2
    node, me = lax.axis_index("node"), lax.axis_index("local")
    hi, lo = me // 2, me % 2
    mate = hi * 2 + (1 - lo)

    def ahead(steps):
        return (lax.rem(node + steps + nodes, nodes), me)

    def beside(index):
        return (node, index)

    def turned(d):
        return lax.rem(hi + d, his)

    fetches = [
        pltpu.make_async_copy(source, dest, wsem.at[i])
        for i, (source, dest) in enumerate((
            (route_hbm, route_ref), (x_hbm, x_ref), (g_hbm, g_ref), (fixed_hbm, fixed_ref),
            (gate_hbm.at[0], gw), (up_hbm.at[0], uw), (down_hbm.at[0], dw),
        ))
    ]
    for copy in fetches:
        copy.start()

    barrier = pltpu.get_barrier_semaphore()
    friends = [ahead(s) for o in range(1, GROUP) for s in (o, -o)]
    friends += [beside(turned(d) * 2 + lo) for d in range(1, his)]
    friends += [beside(mate)]
    for friend in friends:
        pl.semaphore_signal(barrier, inc=1, device_id=friend, device_id_type=MESH)

    def remote(source, dest, send, recv, device):
        return pltpu.make_async_remote_copy(
            src_ref=source, dst_ref=dest, send_sem=send, recv_sem=recv,
            device_id=device, device_id_type=MESH,
        )

    def to_node(o, k):
        return remote(packed.at[o, k], got.at[o, me, k], ns.at[o, k], nr.at[o, k], ahead(o))

    def to_hi(o, k, d):
        return remote(
            got.at[o, me, k], got.at[o, me, k], hs.at[o, k, d], hr.at[o, k, hi],
            beside(turned(d) * 2 + lo),
        )

    def from_hi(o, k, d):
        h = turned(d)
        slot = got.at[o, h * 2 + lo, k]
        return remote(slot, slot, hs.at[o, k, d], hr.at[o, k, h], beside(h * 2 + lo))

    def to_mate(o, k, h):
        slot = got.at[o, h * 2 + lo, k]
        return remote(slot, slot, ls.at[o, k, h], lr.at[o, k, h], beside(mate))

    def from_mate(o, k, h):
        slot = got.at[o, h * 2 + 1 - lo, k]
        return remote(slot, slot, ls.at[o, k, h], lr.at[o, k, h], beside(mate))

    def sum_mate(o, h):
        return remote(out_a.at[o, h], in_a.at[o, h], sa.at[o, h], ra.at[o, h], beside(mate))

    def sum_hi(o, d):
        h = turned(d)
        return remote(out_b.at[o, h], in_b.at[o, hi], sb.at[o, h], rb.at[o, hi], beside(h * 2 + lo))

    def sum_from_hi(o, d):
        h = turned(d)
        return remote(out_b.at[o, h], in_b.at[o, h], sb.at[o, h], rb.at[o, h], beside(h * 2 + lo))

    def to_home(o):
        return remote(out_h.at[o], in_h.at[o], sm.at[o], rm.at[o], ahead(-o))

    def gate_mate(o):
        return remote(gate_out_a.at[o], gate_in_a.at[o], sga.at[o], rga.at[o], beside(mate))

    def gate_hi(o, d):
        h = turned(d)
        return remote(
            gate_out_b.at[o], gate_in_b.at[o, hi], sgb.at[o, h], rgb.at[o, hi], beside(h * 2 + lo)
        )

    def gate_from_hi(o, d):
        h = turned(d)
        return remote(
            gate_out_b.at[o], gate_in_b.at[o, h], sgb.at[o, h], rgb.at[o, h], beside(h * 2 + lo)
        )

    def gate_home(o):
        return remote(gate_out_h.at[o], gate_in_h.at[o], sgm.at[o], rgm.at[o], ahead(-o))

    fetches[0].wait()
    lanes = lax.broadcasted_iota(jnp.int32, (tokens, LANES), 1).astype(jnp.float32)
    routes = [stand_up(route_ref[k:k + 1, :].astype(jnp.float32)) for k in range(2)]
    chosen = ((routes[0] == lanes) | (routes[1] == lanes)).astype(jnp.float32)
    row = lax.broadcasted_iota(jnp.int32, (tokens, tokens), 0)
    column = lax.broadcasted_iota(jnp.int32, (tokens, tokens), 1)
    below = (column <= row).astype(jnp.float32).astype(jnp.bfloat16)
    ranks = dot(below, chosen.astype(jnp.bfloat16))
    slots = lax.broadcasted_iota(jnp.int32, (tokens, CAPACITY), 1).astype(jnp.float32) + 1.0
    tables = []
    for o in range(GROUP):
        here = (ranks[:, o:o + 1] == slots) & (chosen[:, o:o + 1] > 0.5)
        tables.append(here.astype(jnp.float32).astype(jnp.bfloat16))
        table[o] = tables[o]

    def pack(o, k):
        source = x_ref if k == 0 else g_ref
        return dot(tables[o], source[...], TN).astype(jnp.bfloat16)

    fetches[1].wait()
    got[0, me, 0] = pack(0, 0)
    packed[1, 0] = pack(1, 0)
    fetches[2].wait()
    pl.semaphore_wait(barrier, len(friends))
    for d in range(1, his):
        to_hi(0, 0, d).start()
    to_node(1, 0).start()
    got[0, me, 1] = pack(0, 1)
    for d in range(1, his):
        to_hi(0, 1, d).start()
    packed[1, 1] = pack(1, 1)
    to_node(1, 1).start()
    for o in range(2, GROUP):
        for k in range(2):
            packed[o, k] = pack(o, k)
            to_node(o, k).start()
    for k in range(2):
        to_mate(0, k, hi).start()
    for copy in fetches[3:]:
        copy.wait()

    def spread(o):
        for k in range(2):
            to_node(o, k).wait_recv()
            for d in range(1, his):
                to_hi(o, k, d).start()
            to_mate(o, k, hi).start()

    def block(l):
        return pl.ds(pl.multiple_of(l * feat, 64), feat)

    def arrivals(o, k, add):
        add(me)
        from_mate(o, k, hi).wait_recv()
        add(mate)
        for d in range(1, his):
            h = turned(d)
            from_hi(o, k, d).wait_recv()
            to_mate(o, k, h).start()
            add(h * 2 + lo)
            from_mate(o, k, h).wait_recv()
            add(h * 2 + 1 - lo)

    def compute(o):
        sums = [jnp.zeros((CAPACITY, gw.shape[1]), jnp.float32) for _ in range(3)]

        def add_input(l):
            x = got[o, l, 0]
            sums[0] = sums[0] + dot(x, gw[block(l), :])
            sums[1] = sums[1] + dot(x, uw[block(l), :])

        def add_grad(l):
            if feat % LANES == 0:
                rows = pl.ds(pl.multiple_of(l * feat, LANES), feat)
                sums[2] = sums[2] + dot(got[o, l, 1], dw[:, rows], NT)

        arrivals(o, 0, add_input)
        arrivals(o, 1, add_grad)
        if feat % LANES:
            for l in range(locals_):
                sums[2] = sums[2] + dot(got[o, l, 1], dw[:, pl.ds(l * feat, feat)], NT)
        a, b, v = sums
        s = 1.0 / (1.0 + jnp.exp(-a))
        swish = a * s
        u = (v * swish).astype(jnp.bfloat16)
        w = (v * b * s * (1.0 + a * (1.0 - s))).astype(jnp.bfloat16)
        gate_out_a[o] = split_gate(lay_down(jnp.sum(swish * b * v, axis=1, keepdims=True)))
        gate_mate(o).start()

        @pl.when(o >= 1)
        def _():
            add_hi(o - 1)

        def back(l):
            return dot(w, gw[block(l), :], NT) + dot(u, uw[block(l), :], NT)

        def send_mate(h):
            out_a[o, h] = back(h * 2 + 1 - lo).astype(jnp.bfloat16)
            sum_mate(o, h).start()

        def with_mate(h, part):
            sum_mate(o, h).wait_recv()
            return part + in_a[o, h].astype(jnp.float32)

        for d in range(1, his):
            send_mate(turned(d))
        parts = [back(turned(d) * 2 + lo) for d in range(1, his)]
        send_mate(hi)
        for d in range(1, his):
            h = turned(d)
            out_b[o, h] = with_mate(h, parts[d - 1]).astype(jnp.bfloat16)
            sum_hi(o, d).start()
        gate_mate(o).wait_recv()
        gate = split_gate(join_gate(gate_out_a[o]) + join_gate(gate_in_a[o]))
        gate_out_b[o] = gate
        gate_in_b[o, hi] = gate
        for d in range(1, his):
            gate_hi(o, d).start()
        mine[o] = with_mate(hi, back(me))

    def add_hi(o):
        total = mine[o]
        for d in range(1, his):
            sum_from_hi(o, d).wait_recv()
            total = total + in_b[o, turned(d)].astype(jnp.float32)
        out_h[o] = total.astype(jnp.bfloat16)

        @pl.when(o > 0)
        def _():
            to_home(o).start()

        for d in range(1, his):
            gate_from_hi(o, d).wait_recv()
        gate = join_gate(gate_in_b[o, 0])
        for h in range(1, his):
            gate = gate + join_gate(gate_in_b[o, h])
        gate_out_h[o] = split_gate(gate)

        @pl.when(o > 0)
        def _():
            gate_home(o).start()

    def step(i, carry):
        @pl.when(i + 1 < GROUP)
        def _():
            spread(i + 1)

        compute(i)
        return carry

    lax.fori_loop(0, GROUP, step, 0)
    add_hi(GROUP - 1)

    gates = [stand_up(fixed_ref[k:k + 1, :].astype(jnp.float32)) / 65536.0 for k in range(2)]
    total = jnp.zeros((tokens, feat), jnp.float32)
    gate_total = [jnp.zeros((tokens, LANES), jnp.float32) for _ in range(2)]
    for o in range(GROUP):
        if o > 0:
            to_home(o).wait_recv()
        home = out_h if o == 0 else in_h
        hits = [routes[k] == float(o) for k in range(2)]
        weight = sum(jnp.where(hits[k], gates[k], 0.0) for k in range(2))[:, 0:1]
        total = total + weight * dot(table[o], home[o])
    for o in range(GROUP):
        if o > 0:
            gate_home(o).wait_recv()
        home = gate_out_h if o == 0 else gate_in_h
        pair = dot(table[o], home[o][:, 0:CAPACITY], NT)
        value = pair[:, 0:1] + pair[:, 8:9]
        for k in range(2):
            gate_total[k] = gate_total[k] + jnp.where(routes[k] == float(o), value, 0.0)
    out_ref[...] = total.astype(jnp.bfloat16)
    for k in range(2):
        ggrad_ref[k:k + 1, :] = gate_total[k].T[0:1]

    def finish(o, carry):
        for k in range(2):
            for d in range(1, his):
                to_hi(o, k, d).wait_send()
            for h in range(his):
                to_mate(o, k, h).wait_send()
        gate_mate(o).wait_send()
        for h in range(his):
            sum_mate(o, h).wait_send()
        for d in range(1, his):
            sum_hi(o, d).wait_send()
            gate_hi(o, d).wait_send()

        @pl.when(o > 0)
        def _():
            for k in range(2):
                to_node(o, k).wait_send()
            to_home(o).wait_send()
            gate_home(o).wait_send()

        return carry

    lax.fori_loop(0, GROUP, finish, 0)


def body(nodes, locals_, layer_input, output_grad, gate_weight, up_weight, down_weight, route, fixed):
    tokens, feat = layer_input.shape
    width, hidden = gate_weight.shape[1:]
    his = locals_ // 2
    bf16, f32, i32 = jnp.bfloat16, jnp.float32, jnp.int32
    vmem, dma = pltpu.VMEM, pltpu.SemaphoreType.DMA
    routed = GROUP * CAPACITY
    scratch = [
        vmem((tokens, feat), bf16),
        vmem((tokens, feat), bf16),
        vmem((width, hidden), bf16),
        vmem((width, hidden), bf16),
        vmem((hidden, width), bf16),
        vmem((2, tokens), i32),
        vmem((2, tokens), i32),
        vmem((GROUP, tokens, CAPACITY), bf16),
        vmem((GROUP, 2, CAPACITY, feat), bf16),
        vmem((GROUP, locals_, 2, CAPACITY, feat), bf16),
        vmem((GROUP, his, CAPACITY, feat), bf16),
        vmem((GROUP, his, CAPACITY, feat), bf16),
        vmem((GROUP, his, CAPACITY, feat), bf16),
        vmem((GROUP, his, CAPACITY, feat), bf16),
        vmem((GROUP, CAPACITY, feat), f32),
        vmem((GROUP, CAPACITY, feat), bf16),
        vmem((GROUP, CAPACITY, feat), bf16),
        vmem((GROUP, 16, LANES), bf16),
        vmem((GROUP, 16, LANES), bf16),
        vmem((GROUP, 16, LANES), bf16),
        vmem((GROUP, his, 16, LANES), bf16),
        vmem((GROUP, 16, LANES), bf16),
        vmem((GROUP, 16, LANES), bf16),
        dma((7,)),
        dma((GROUP, 2)),
        dma((GROUP, 2)),
        dma((GROUP, 2, his)),
        dma((GROUP, 2, his)),
        dma((GROUP, 2, his)),
        dma((GROUP, 2, his)),
        dma((GROUP, his)),
        dma((GROUP, his)),
        dma((GROUP, his)),
        dma((GROUP, his)),
        dma((GROUP,)),
        dma((GROUP,)),
        dma((GROUP,)),
        dma((GROUP,)),
        dma((GROUP, his)),
        dma((GROUP, his)),
        dma((GROUP,)),
        dma((GROUP,)),
    ]
    in_vmem, anywhere = pl.BlockSpec(memory_space=pltpu.VMEM), pl.BlockSpec(memory_space=pl.ANY)
    grads, gate_grads = pl.pallas_call(
        functools.partial(kernel, nodes, locals_),
        out_shape=(
            jax.ShapeDtypeStruct((tokens, feat), bf16),
            jax.ShapeDtypeStruct((2, tokens), f32),
        ),
        in_specs=[anywhere] * 7,
        out_specs=(in_vmem, in_vmem),
        scratch_shapes=scratch,
        compiler_params=pltpu.CompilerParams(
            collective_id=0, has_side_effects=True, vmem_limit_bytes=60 * 1024 * 1024
        ),
        cost_estimate=pl.CostEstimate(
            flops=10 * routed * width * hidden,
            bytes_accessed=6 * width * hidden + 6 * tokens * feat,
            transcendentals=routed * hidden,
        ),
    )(layer_input, output_grad, gate_weight, up_weight, down_weight, route.T, fixed.T)
    return grads, gate_grads.T


def solution(mesh):
    in_specs = (
        P("node", "local"),
        P("node", "local"),
        P("node", None, "local"),
        P("node", None, "local"),
        P("node", "local", None),
        P("node", None),
        P("node", None),
    )
    out_specs = (P("node", "local"), P("node", None))
    run = functools.partial(body, mesh.shape["node"], mesh.shape["local"])
    return jax.shard_map(run, mesh=mesh, in_specs=in_specs, out_specs=out_specs, check_vma=False)
```

```python
import functools

import jax
import jax.numpy as jnp
from jax import lax
from jax.experimental import pallas as pl
from jax.experimental.pallas import tpu as pltpu
from jax.sharding import PartitionSpec as P

GROUP = 4
CAPACITY = 80
ORDER = (0, 2, 3, 1)
LANES = 128
MESH = pl.DeviceIdType.MESH
NT = (((1,), (1,)), ((), ()))
TN = (((0,), (0,)), ((), ()))


def dot(a, b, dims=None):
    if dims is None:
        return jnp.dot(a, b, preferred_element_type=jnp.float32)
    return lax.dot_general(a, b, dims, preferred_element_type=jnp.float32)


def split_gate(value):
    high = value.astype(jnp.bfloat16).astype(jnp.float32)
    return jnp.concatenate((high, value - high), axis=0).astype(jnp.bfloat16)


def join_gate(parts):
    parts = parts.astype(jnp.float32)
    return parts[0:8] + parts[8:16]


def lay_down(column):
    wide = jnp.broadcast_to(column, (CAPACITY, LANES))
    rest = jnp.zeros((LANES - CAPACITY, LANES), jnp.float32)
    return jnp.concatenate((wide, rest), axis=0).T[0:8]


def stand_up(row):
    return jnp.broadcast_to(row, (LANES, row.shape[1])).T


def kernel(
    nodes, locals_,
    x_hbm, g_hbm, gate_hbm, up_hbm, down_hbm, route_hbm, fixed_hbm,
    out_ref, ggrad_ref,
    x_ref, g_ref, gw, uw, dw, route_ref, fixed_ref,
    table, packed, got, out_a, in_a, out_b, in_b, mine, out_h, in_h,
    gate_out_a, gate_in_a, gate_out_b, gate_in_b, gate_out_h, gate_in_h,
    wsem, ns, nr, hs, hr, ls, lr, sa, ra, sb, rb, sm, rm, sga, rga, sgb, rgb, sgm, rgm,
):
    tokens, feat = x_ref.shape
    his = locals_ // 2
    node, me = lax.axis_index("node"), lax.axis_index("local")
    hi, lo = me // 2, me % 2
    mate = hi * 2 + (1 - lo)

    def ahead(steps):
        return (lax.rem(node + steps + nodes, nodes), me)

    def beside(index):
        return (node, index)

    def offset(p):
        return (p % 3 + 1) * ((p + 3) // 4)

    def turned(d):
        return lax.rem(hi + d, his)

    fetches = [
        pltpu.make_async_copy(source, dest, wsem.at[i])
        for i, (source, dest) in enumerate((
            (route_hbm, route_ref), (x_hbm, x_ref), (g_hbm, g_ref), (fixed_hbm, fixed_ref),
            (gate_hbm.at[0], gw), (up_hbm.at[0], uw), (down_hbm.at[0], dw),
        ))
    ]
    for copy in fetches:
        copy.start()

    barrier = pltpu.get_barrier_semaphore()
    friends = [ahead(s) for o in range(1, GROUP) for s in (o, -o)]
    friends += [beside(turned(d) * 2 + lo) for d in range(1, his)]
    friends += [beside(mate)]
    for friend in friends:
        pl.semaphore_signal(barrier, inc=1, device_id=friend, device_id_type=MESH)

    def remote(source, dest, send, recv, device):
        return pltpu.make_async_remote_copy(
            src_ref=source, dst_ref=dest, send_sem=send, recv_sem=recv,
            device_id=device, device_id_type=MESH,
        )

    def to_node(o, k):
        return remote(packed.at[o, k], got.at[o, me, k], ns.at[o, k], nr.at[o, k], ahead(offset(o)))

    def to_hi(o, k, d):
        return remote(
            got.at[o, me, k], got.at[o, me, k], hs.at[o, k, d], hr.at[o, k, hi],
            beside(turned(d) * 2 + lo),
        )

    def from_hi(o, k, d):
        h = turned(d)
        slot = got.at[o, h * 2 + lo, k]
        return remote(slot, slot, hs.at[o, k, d], hr.at[o, k, h], beside(h * 2 + lo))

    def to_mate(o, k, h):
        slot = got.at[o, h * 2 + lo, k]
        return remote(slot, slot, ls.at[o, k, h], lr.at[o, k, h], beside(mate))

    def from_mate(o, k, h):
        slot = got.at[o, h * 2 + 1 - lo, k]
        return remote(slot, slot, ls.at[o, k, h], lr.at[o, k, h], beside(mate))

    def sum_mate(o, h):
        return remote(out_a.at[o, h], in_a.at[o, h], sa.at[o, h], ra.at[o, h], beside(mate))

    def sum_hi(o, d):
        h = turned(d)
        return remote(out_b.at[o, h], in_b.at[o, hi], sb.at[o, h], rb.at[o, hi], beside(h * 2 + lo))

    def sum_from_hi(o, d):
        h = turned(d)
        return remote(out_b.at[o, h], in_b.at[o, h], sb.at[o, h], rb.at[o, h], beside(h * 2 + lo))

    def to_home(o):
        return remote(out_h.at[o], in_h.at[o], sm.at[o], rm.at[o], ahead(-offset(o)))

    def gate_mate(o):
        return remote(gate_out_a.at[o], gate_in_a.at[o], sga.at[o], rga.at[o], beside(mate))

    def gate_hi(o, d):
        h = turned(d)
        return remote(
            gate_out_b.at[o], gate_in_b.at[o, hi], sgb.at[o, h], rgb.at[o, hi], beside(h * 2 + lo)
        )

    def gate_from_hi(o, d):
        h = turned(d)
        return remote(
            gate_out_b.at[o], gate_in_b.at[o, h], sgb.at[o, h], rgb.at[o, h], beside(h * 2 + lo)
        )

    def gate_home(o):
        return remote(gate_out_h.at[o], gate_in_h.at[o], sgm.at[o], rgm.at[o], ahead(-offset(o)))

    fetches[0].wait()
    lanes = lax.broadcasted_iota(jnp.int32, (tokens, LANES), 1).astype(jnp.float32)
    routes = [stand_up(route_ref[k:k + 1, :].astype(jnp.float32)) for k in range(2)]
    chosen = ((routes[0] == lanes) | (routes[1] == lanes)).astype(jnp.float32)
    row = lax.broadcasted_iota(jnp.int32, (tokens, tokens), 0)
    column = lax.broadcasted_iota(jnp.int32, (tokens, tokens), 1)
    below = (column <= row).astype(jnp.float32).astype(jnp.bfloat16)
    ranks = dot(below, chosen.astype(jnp.bfloat16))
    slots = lax.broadcasted_iota(jnp.int32, (tokens, CAPACITY), 1).astype(jnp.float32) + 1.0
    tables = []
    for o in range(GROUP):
        at = slice(ORDER[o], ORDER[o] + 1)
        here = (ranks[:, at] == slots) & (chosen[:, at] > 0.5)
        tables.append(here.astype(jnp.float32).astype(jnp.bfloat16))
        table[o] = tables[o]

    def pack(o, k):
        source = x_ref if k == 0 else g_ref
        return dot(tables[o], source[...], TN).astype(jnp.bfloat16)

    fetches[1].wait()
    got[0, me, 0] = pack(0, 0)
    packed[1, 0] = pack(1, 0)
    fetches[2].wait()
    pl.semaphore_wait(barrier, len(friends))
    for d in range(1, his):
        to_hi(0, 0, d).start()
    to_node(1, 0).start()
    got[0, me, 1] = pack(0, 1)
    for d in range(1, his):
        to_hi(0, 1, d).start()
    packed[1, 1] = pack(1, 1)
    to_node(1, 1).start()
    for k in range(2):
        to_mate(0, k, hi).start()
    for o in range(2, GROUP):
        for k in range(2):
            packed[o, k] = pack(o, k)
    for copy in fetches[3:]:
        copy.wait()

    def spread(o):
        for k in range(2):
            to_node(o, k).wait_send()

            @pl.when(o + 1 < GROUP)
            def _():
                to_node(o + 1, k).start()

            to_node(o, k).wait_recv()
            for d in range(1, his):
                to_hi(o, k, d).start()
            to_mate(o, k, hi).start()

    def block(l):
        return pl.ds(pl.multiple_of(l * feat, 64), feat)

    def arrivals(o, k, add):
        add(me)
        from_mate(o, k, hi).wait_recv()
        add(mate)
        for d in range(1, his):
            h = turned(d)
            from_hi(o, k, d).wait_recv()
            to_mate(o, k, h).start()
            add(h * 2 + lo)
            from_mate(o, k, h).wait_recv()
            add(h * 2 + 1 - lo)

    def compute(o):
        sums = [jnp.zeros((CAPACITY, gw.shape[1]), jnp.float32) for _ in range(3)]

        def add_input(l):
            x = got[o, l, 0]
            sums[0] = sums[0] + dot(x, gw[block(l), :])
            sums[1] = sums[1] + dot(x, uw[block(l), :])

        def add_grad(l):
            if feat % LANES == 0:
                rows = pl.ds(pl.multiple_of(l * feat, LANES), feat)
                sums[2] = sums[2] + dot(got[o, l, 1], dw[:, rows], NT)

        arrivals(o, 0, add_input)
        arrivals(o, 1, add_grad)
        if feat % LANES:
            for l in range(locals_):
                sums[2] = sums[2] + dot(got[o, l, 1], dw[:, pl.ds(l * feat, feat)], NT)
        a, b, v = sums
        s = 1.0 / (1.0 + jnp.exp(-a))
        swish = a * s
        u = (v * swish).astype(jnp.bfloat16)
        w = (v * b * s * (1.0 + a * (1.0 - s))).astype(jnp.bfloat16)
        gate_out_a[o] = split_gate(lay_down(jnp.sum(swish * b * v, axis=1, keepdims=True)))
        gate_mate(o).start()

        @pl.when(o >= 1)
        def _():
            add_hi(o - 1)

        def back(l):
            return dot(w, gw[block(l), :], NT) + dot(u, uw[block(l), :], NT)

        def send_mate(h):
            out_a[o, h] = back(h * 2 + 1 - lo).astype(jnp.bfloat16)
            sum_mate(o, h).start()

        def with_mate(h, part):
            sum_mate(o, h).wait_recv()
            return part + in_a[o, h].astype(jnp.float32)

        for d in range(1, his):
            send_mate(turned(d))
        parts = [back(turned(d) * 2 + lo) for d in range(1, his)]
        send_mate(hi)
        for d in range(1, his):
            h = turned(d)
            out_b[o, h] = with_mate(h, parts[d - 1]).astype(jnp.bfloat16)
            sum_hi(o, d).start()
        gate_mate(o).wait_recv()
        gate = split_gate(join_gate(gate_out_a[o]) + join_gate(gate_in_a[o]))
        gate_out_b[o] = gate
        gate_in_b[o, hi] = gate
        for d in range(1, his):
            gate_hi(o, d).start()
        mine[o] = with_mate(hi, back(me))

    def add_hi(o):
        total = mine[o]
        for d in range(1, his):
            sum_from_hi(o, d).wait_recv()
            total = total + in_b[o, turned(d)].astype(jnp.float32)
        out_h[o] = total.astype(jnp.bfloat16)

        @pl.when(o > 0)
        def _():
            to_home(o).start()

        for d in range(1, his):
            gate_from_hi(o, d).wait_recv()
        gate = join_gate(gate_in_b[o, 0])
        for h in range(1, his):
            gate = gate + join_gate(gate_in_b[o, h])
        gate_out_h[o] = split_gate(gate)

        @pl.when(o > 0)
        def _():
            gate_home(o).start()

    def step(i, carry):
        @pl.when(i + 1 < GROUP)
        def _():
            spread(i + 1)

        compute(i)
        return carry

    lax.fori_loop(0, GROUP, step, 0)
    add_hi(GROUP - 1)

    gates = [stand_up(fixed_ref[k:k + 1, :].astype(jnp.float32)) / 65536.0 for k in range(2)]
    total = jnp.zeros((tokens, feat), jnp.float32)
    gate_total = [jnp.zeros((tokens, LANES), jnp.float32) for _ in range(2)]
    for o in range(GROUP):
        if o > 0:
            to_home(o).wait_recv()
        home = out_h if o == 0 else in_h
        hits = [routes[k] == float(ORDER[o]) for k in range(2)]
        weight = sum(jnp.where(hits[k], gates[k], 0.0) for k in range(2))[:, 0:1]
        total = total + weight * dot(table[o], home[o])
    for o in range(GROUP):
        if o > 0:
            gate_home(o).wait_recv()
        home = gate_out_h if o == 0 else gate_in_h
        pair = dot(table[o], home[o][:, 0:CAPACITY], NT)
        value = pair[:, 0:1] + pair[:, 8:9]
        for k in range(2):
            gate_total[k] = gate_total[k] + jnp.where(routes[k] == float(ORDER[o]), value, 0.0)
    out_ref[...] = total.astype(jnp.bfloat16)
    for k in range(2):
        ggrad_ref[k:k + 1, :] = gate_total[k].T[0:1]

    def finish(o, carry):
        for k in range(2):
            for d in range(1, his):
                to_hi(o, k, d).wait_send()
            for h in range(his):
                to_mate(o, k, h).wait_send()
        gate_mate(o).wait_send()
        for h in range(his):
            sum_mate(o, h).wait_send()
        for d in range(1, his):
            sum_hi(o, d).wait_send()
            gate_hi(o, d).wait_send()

        @pl.when(o > 0)
        def _():
            to_home(o).wait_send()
            gate_home(o).wait_send()

        return carry

    lax.fori_loop(0, GROUP, finish, 0)


def body(nodes, locals_, layer_input, output_grad, gate_weight, up_weight, down_weight, route, fixed):
    tokens, feat = layer_input.shape
    width, hidden = gate_weight.shape[1:]
    his = locals_ // 2
    bf16, f32, i32 = jnp.bfloat16, jnp.float32, jnp.int32
    vmem, dma = pltpu.VMEM, pltpu.SemaphoreType.DMA
    routed = GROUP * CAPACITY
    scratch = [
        vmem((tokens, feat), bf16),
        vmem((tokens, feat), bf16),
        vmem((width, hidden), bf16),
        vmem((width, hidden), bf16),
        vmem((hidden, width), bf16),
        vmem((2, tokens), i32),
        vmem((2, tokens), i32),
        vmem((GROUP, tokens, CAPACITY), bf16),
        vmem((GROUP, 2, CAPACITY, feat), bf16),
        vmem((GROUP, locals_, 2, CAPACITY, feat), bf16),
        vmem((GROUP, his, CAPACITY, feat), bf16),
        vmem((GROUP, his, CAPACITY, feat), bf16),
        vmem((GROUP, his, CAPACITY, feat), bf16),
        vmem((GROUP, his, CAPACITY, feat), bf16),
        vmem((GROUP, CAPACITY, feat), f32),
        vmem((GROUP, CAPACITY, feat), bf16),
        vmem((GROUP, CAPACITY, feat), bf16),
        vmem((GROUP, 16, LANES), bf16),
        vmem((GROUP, 16, LANES), bf16),
        vmem((GROUP, 16, LANES), bf16),
        vmem((GROUP, his, 16, LANES), bf16),
        vmem((GROUP, 16, LANES), bf16),
        vmem((GROUP, 16, LANES), bf16),
        dma((7,)),
        dma((GROUP, 2)),
        dma((GROUP, 2)),
        dma((GROUP, 2, his)),
        dma((GROUP, 2, his)),
        dma((GROUP, 2, his)),
        dma((GROUP, 2, his)),
        dma((GROUP, his)),
        dma((GROUP, his)),
        dma((GROUP, his)),
        dma((GROUP, his)),
        dma((GROUP,)),
        dma((GROUP,)),
        dma((GROUP,)),
        dma((GROUP,)),
        dma((GROUP, his)),
        dma((GROUP, his)),
        dma((GROUP,)),
        dma((GROUP,)),
    ]
    in_vmem, anywhere = pl.BlockSpec(memory_space=pltpu.VMEM), pl.BlockSpec(memory_space=pl.ANY)
    grads, gate_grads = pl.pallas_call(
        functools.partial(kernel, nodes, locals_),
        out_shape=(
            jax.ShapeDtypeStruct((tokens, feat), bf16),
            jax.ShapeDtypeStruct((2, tokens), f32),
        ),
        in_specs=[anywhere] * 7,
        out_specs=(in_vmem, in_vmem),
        scratch_shapes=scratch,
        compiler_params=pltpu.CompilerParams(
            collective_id=0, has_side_effects=True, vmem_limit_bytes=48 * 1024 * 1024
        ),
        cost_estimate=pl.CostEstimate(
            flops=10 * routed * width * hidden,
            bytes_accessed=6 * width * hidden + 6 * tokens * feat,
            transcendentals=routed * hidden,
        ),
    )(layer_input, output_grad, gate_weight, up_weight, down_weight, route.T, fixed.T)
    return grads, gate_grads.T


def solution(mesh):
    in_specs = (
        P("node", "local"),
        P("node", "local"),
        P("node", None, "local"),
        P("node", None, "local"),
        P("node", "local", None),
        P("node", None),
        P("node", None),
    )
    out_specs = (P("node", "local"), P("node", None))
    run = functools.partial(body, mesh.shape["node"], mesh.shape["local"])
    return jax.shard_map(run, mesh=mesh, in_specs=in_specs, out_specs=out_specs, check_vma=False)
```

```python
import functools

import jax
import jax.numpy as jnp
from jax import lax
from jax.experimental import pallas as pl
from jax.experimental.pallas import tpu as pltpu
from jax.sharding import PartitionSpec as P

GROUP = 4
CAPACITY = 80
LANES = 128
MESH = pl.DeviceIdType.MESH
NT = (((1,), (1,)), ((), ()))
TN = (((0,), (0,)), ((), ()))


def dot(a, b, dims=None):
    if dims is None:
        return jnp.dot(a, b, preferred_element_type=jnp.float32)
    return lax.dot_general(a, b, dims, preferred_element_type=jnp.float32)


def split_gate(value):
    high = value.astype(jnp.bfloat16).astype(jnp.float32)
    return jnp.concatenate((high, value - high), axis=0).astype(jnp.bfloat16)


def join_gate(parts):
    parts = parts.astype(jnp.float32)
    return parts[0:8] + parts[8:16]


def lay_down(column):
    wide = jnp.broadcast_to(column, (CAPACITY, LANES))
    rest = jnp.zeros((LANES - CAPACITY, LANES), jnp.float32)
    return jnp.concatenate((wide, rest), axis=0).T[0:8]


def stand_up(row):
    return jnp.broadcast_to(row, (LANES, row.shape[1])).T


def kernel(
    nodes, locals_,
    x_hbm, g_hbm, gate_hbm, up_hbm, down_hbm, route_hbm, fixed_hbm,
    out_ref, ggrad_ref,
    x_ref, g_ref, gw, uw, dw, route_ref, fixed_ref,
    table, packed, got, out_a, in_a, out_b, in_b, mine, out_h, in_h,
    gate_out_a, gate_in_a, gate_out_b, gate_in_b, gate_out_h, gate_in_h,
    relay,
    wsem, es, er, ns, nr, hs, hr, ls, lr, sa, ra, sb, rb, sm, rm, sga, rga, sgb, rgb, sgm, rgm,
):
    tokens, feat = x_ref.shape
    his = locals_ // 2
    node, me = lax.axis_index("node"), lax.axis_index("local")
    hi, lo = me // 2, me % 2
    mate = hi * 2 + (1 - lo)

    def ahead(steps):
        return (lax.rem(node + steps + nodes, nodes), me)

    def beside(index):
        return (node, index)

    def turned(d):
        return lax.rem(hi + d, his)

    fetches = [
        pltpu.make_async_copy(source, dest, wsem.at[i])
        for i, (source, dest) in enumerate((
            (route_hbm, route_ref), (x_hbm, x_ref), (g_hbm, g_ref), (fixed_hbm, fixed_ref),
            (gate_hbm.at[0], gw), (up_hbm.at[0], uw), (down_hbm.at[0], dw),
        ))
    ]
    for copy in fetches:
        copy.start()

    barrier = pltpu.get_barrier_semaphore()
    friends = [ahead(s) for o in range(1, GROUP) for s in (o, -o)]
    friends += [beside(turned(d) * 2 + lo) for d in range(1, his)]
    friends += [beside(mate)]
    for friend in friends:
        pl.semaphore_signal(barrier, inc=1, device_id=friend, device_id_type=MESH)

    def remote(source, dest, send, recv, device):
        return pltpu.make_async_remote_copy(
            src_ref=source, dst_ref=dest, send_sem=send, recv_sem=recv,
            device_id=device, device_id_type=MESH,
        )

    def to_node(o, k):
        return remote(packed.at[o, k], got.at[o, me, k], ns.at[o, k], nr.at[o, k], ahead(o))

    far = GROUP - 1
    legs = nodes % 2 == 0
    odd = lax.rem(node, 2) == 1

    def first_leg(k):
        return remote(packed.at[far, k], relay.at[k], es.at[k], er.at[k], ahead(1))

    def second_leg(k):
        return remote(
            relay.at[k], got.at[far, me, k], es.at[k], nr.at[far, k], ahead(far - 1)
        )

    def pass_legs():
        if legs:
            @pl.when(jnp.logical_not(odd))
            def _():
                for k in range(2):
                    first_leg(k).wait_recv()
                    second_leg(k).start()

    def to_hi(o, k, d):
        return remote(
            got.at[o, me, k], got.at[o, me, k], hs.at[o, k, d], hr.at[o, k, hi],
            beside(turned(d) * 2 + lo),
        )

    def from_hi(o, k, d):
        h = turned(d)
        slot = got.at[o, h * 2 + lo, k]
        return remote(slot, slot, hs.at[o, k, d], hr.at[o, k, h], beside(h * 2 + lo))

    def to_mate(o, k, h):
        slot = got.at[o, h * 2 + lo, k]
        return remote(slot, slot, ls.at[o, k, h], lr.at[o, k, h], beside(mate))

    def from_mate(o, k, h):
        slot = got.at[o, h * 2 + 1 - lo, k]
        return remote(slot, slot, ls.at[o, k, h], lr.at[o, k, h], beside(mate))

    def sum_mate(o, h):
        return remote(out_a.at[o, h], in_a.at[o, h], sa.at[o, h], ra.at[o, h], beside(mate))

    def sum_hi(o, d):
        h = turned(d)
        return remote(out_b.at[o, h], in_b.at[o, hi], sb.at[o, h], rb.at[o, hi], beside(h * 2 + lo))

    def sum_from_hi(o, d):
        h = turned(d)
        return remote(out_b.at[o, h], in_b.at[o, h], sb.at[o, h], rb.at[o, h], beside(h * 2 + lo))

    def to_home(o):
        return remote(out_h.at[o], in_h.at[o], sm.at[o], rm.at[o], ahead(-o))

    def gate_mate(o):
        return remote(gate_out_a.at[o], gate_in_a.at[o], sga.at[o], rga.at[o], beside(mate))

    def gate_hi(o, d):
        h = turned(d)
        return remote(
            gate_out_b.at[o], gate_in_b.at[o, hi], sgb.at[o, h], rgb.at[o, hi], beside(h * 2 + lo)
        )

    def gate_from_hi(o, d):
        h = turned(d)
        return remote(
            gate_out_b.at[o], gate_in_b.at[o, h], sgb.at[o, h], rgb.at[o, h], beside(h * 2 + lo)
        )

    def gate_home(o):
        return remote(gate_out_h.at[o], gate_in_h.at[o], sgm.at[o], rgm.at[o], ahead(-o))

    fetches[0].wait()
    lanes = lax.broadcasted_iota(jnp.int32, (tokens, LANES), 1).astype(jnp.float32)
    routes = [stand_up(route_ref[k:k + 1, :].astype(jnp.float32)) for k in range(2)]
    chosen = ((routes[0] == lanes) | (routes[1] == lanes)).astype(jnp.float32)
    row = lax.broadcasted_iota(jnp.int32, (tokens, tokens), 0)
    column = lax.broadcasted_iota(jnp.int32, (tokens, tokens), 1)
    below = (column <= row).astype(jnp.float32).astype(jnp.bfloat16)
    ranks = dot(below, chosen.astype(jnp.bfloat16))
    slots = lax.broadcasted_iota(jnp.int32, (tokens, CAPACITY), 1).astype(jnp.float32) + 1.0
    tables = []
    for o in range(GROUP):
        here = (ranks[:, o:o + 1] == slots) & (chosen[:, o:o + 1] > 0.5)
        tables.append(here.astype(jnp.float32).astype(jnp.bfloat16))
        table[o] = tables[o]

    def pack(o, k):
        source = x_ref if k == 0 else g_ref
        return dot(tables[o], source[...], TN).astype(jnp.bfloat16)

    fetches[1].wait()
    got[0, me, 0] = pack(0, 0)
    packed[far, 0] = pack(far, 0)
    packed[1, 0] = pack(1, 0)
    fetches[2].wait()
    pl.semaphore_wait(barrier, len(friends))

    def first_sends(k):
        for d in range(1, his):
            to_hi(0, k, d).start()
        if legs:
            @pl.when(odd)
            def _():
                first_leg(k).start()

        to_node(1, k).start()

    first_sends(0)
    got[0, me, 1] = pack(0, 1)
    packed[far, 1] = pack(far, 1)
    packed[1, 1] = pack(1, 1)
    first_sends(1)
    for o in range(2, far):
        for k in range(2):
            packed[o, k] = pack(o, k)
            to_node(o, k).start()
    for k in range(2):
        if legs:
            @pl.when(jnp.logical_not(odd))
            def _():
                to_node(far, k).start()
        else:
            to_node(far, k).start()
    for k in range(2):
        to_mate(0, k, hi).start()
    for copy in fetches[3:]:
        copy.wait()

    def spread(o):
        for k in range(2):
            to_node(o, k).wait_recv()
            for d in range(1, his):
                to_hi(o, k, d).start()
            to_mate(o, k, hi).start()

    def block(l):
        return pl.ds(pl.multiple_of(l * feat, 64), feat)

    def arrivals(o, k, add):
        add(me)
        from_mate(o, k, hi).wait_recv()
        add(mate)
        for d in range(1, his):
            h = turned(d)
            from_hi(o, k, d).wait_recv()
            to_mate(o, k, h).start()
            add(h * 2 + lo)
            from_mate(o, k, h).wait_recv()
            add(h * 2 + 1 - lo)

    def compute(o):
        sums = [jnp.zeros((CAPACITY, gw.shape[1]), jnp.float32) for _ in range(3)]

        def add_input(l):
            x = got[o, l, 0]
            sums[0] = sums[0] + dot(x, gw[block(l), :])
            sums[1] = sums[1] + dot(x, uw[block(l), :])

        def add_grad(l):
            if feat % LANES == 0:
                rows = pl.ds(pl.multiple_of(l * feat, LANES), feat)
                sums[2] = sums[2] + dot(got[o, l, 1], dw[:, rows], NT)

        arrivals(o, 0, add_input)
        arrivals(o, 1, add_grad)
        if feat % LANES:
            for l in range(locals_):
                sums[2] = sums[2] + dot(got[o, l, 1], dw[:, pl.ds(l * feat, feat)], NT)
        a, b, v = sums
        s = 1.0 / (1.0 + jnp.exp(-a))
        swish = a * s
        u = (v * swish).astype(jnp.bfloat16)
        w = (v * b * s * (1.0 + a * (1.0 - s))).astype(jnp.bfloat16)
        gate_out_a[o] = split_gate(lay_down(jnp.sum(swish * b * v, axis=1, keepdims=True)))
        gate_mate(o).start()

        @pl.when(o >= 1)
        def _():
            add_hi(o - 1)

        def back(l):
            return dot(w, gw[block(l), :], NT) + dot(u, uw[block(l), :], NT)

        def send_mate(h):
            out_a[o, h] = back(h * 2 + 1 - lo).astype(jnp.bfloat16)
            sum_mate(o, h).start()

        def with_mate(h, part):
            sum_mate(o, h).wait_recv()
            return part + in_a[o, h].astype(jnp.float32)

        for d in range(1, his):
            send_mate(turned(d))
        parts = [back(turned(d) * 2 + lo) for d in range(1, his)]
        send_mate(hi)
        for d in range(1, his):
            h = turned(d)
            out_b[o, h] = with_mate(h, parts[d - 1]).astype(jnp.bfloat16)
            sum_hi(o, d).start()
        gate_mate(o).wait_recv()
        gate = split_gate(join_gate(gate_out_a[o]) + join_gate(gate_in_a[o]))
        gate_out_b[o] = gate
        gate_in_b[o, hi] = gate
        for d in range(1, his):
            gate_hi(o, d).start()
        mine[o] = with_mate(hi, back(me))

    def add_hi(o):
        total = mine[o]
        for d in range(1, his):
            sum_from_hi(o, d).wait_recv()
            total = total + in_b[o, turned(d)].astype(jnp.float32)
        out_h[o] = total.astype(jnp.bfloat16)

        @pl.when(o > 0)
        def _():
            to_home(o).start()

        for d in range(1, his):
            gate_from_hi(o, d).wait_recv()
        gate = join_gate(gate_in_b[o, 0])
        for h in range(1, his):
            gate = gate + join_gate(gate_in_b[o, h])
        gate_out_h[o] = split_gate(gate)

        @pl.when(o > 0)
        def _():
            gate_home(o).start()

    def step(i, carry):
        @pl.when(i + 1 < GROUP)
        def _():
            spread(i + 1)

        @pl.when(i == 0)
        def _():
            pass_legs()

        compute(i)
        return carry

    lax.fori_loop(0, GROUP, step, 0)
    add_hi(GROUP - 1)

    gates = [stand_up(fixed_ref[k:k + 1, :].astype(jnp.float32)) / 65536.0 for k in range(2)]
    total = jnp.zeros((tokens, feat), jnp.float32)
    gate_total = [jnp.zeros((tokens, LANES), jnp.float32) for _ in range(2)]
    for o in range(GROUP):
        if o > 0:
            to_home(o).wait_recv()
        home = out_h if o == 0 else in_h
        hits = [routes[k] == float(o) for k in range(2)]
        weight = sum(jnp.where(hits[k], gates[k], 0.0) for k in range(2))[:, 0:1]
        total = total + weight * dot(table[o], home[o])
    for o in range(GROUP):
        if o > 0:
            gate_home(o).wait_recv()
        home = gate_out_h if o == 0 else gate_in_h
        pair = dot(table[o], home[o][:, 0:CAPACITY], NT)
        value = pair[:, 0:1] + pair[:, 8:9]
        for k in range(2):
            gate_total[k] = gate_total[k] + jnp.where(routes[k] == float(o), value, 0.0)
    out_ref[...] = total.astype(jnp.bfloat16)
    for k in range(2):
        ggrad_ref[k:k + 1, :] = gate_total[k].T[0:1]

    def finish(o, carry):
        for k in range(2):
            for d in range(1, his):
                to_hi(o, k, d).wait_send()
            for h in range(his):
                to_mate(o, k, h).wait_send()
        gate_mate(o).wait_send()
        for h in range(his):
            sum_mate(o, h).wait_send()
        for d in range(1, his):
            sum_hi(o, d).wait_send()
            gate_hi(o, d).wait_send()

        @pl.when((o > 0) & (o < far))
        def _():
            for k in range(2):
                to_node(o, k).wait_send()

        @pl.when(o > 0)
        def _():
            to_home(o).wait_send()
            gate_home(o).wait_send()

        return carry

    lax.fori_loop(0, GROUP, finish, 0)
    for k in range(2):
        if legs:
            @pl.when(odd)
            def _():
                first_leg(k).wait_send()

            @pl.when(jnp.logical_not(odd))
            def _():
                second_leg(k).wait_send()
                to_node(far, k).wait_send()
        else:
            to_node(far, k).wait_send()


def body(nodes, locals_, layer_input, output_grad, gate_weight, up_weight, down_weight, route, fixed):
    tokens, feat = layer_input.shape
    width, hidden = gate_weight.shape[1:]
    his = locals_ // 2
    bf16, f32, i32 = jnp.bfloat16, jnp.float32, jnp.int32
    vmem, dma = pltpu.VMEM, pltpu.SemaphoreType.DMA
    routed = GROUP * CAPACITY
    scratch = [
        vmem((tokens, feat), bf16),
        vmem((tokens, feat), bf16),
        vmem((width, hidden), bf16),
        vmem((width, hidden), bf16),
        vmem((hidden, width), bf16),
        vmem((2, tokens), i32),
        vmem((2, tokens), i32),
        vmem((GROUP, tokens, CAPACITY), bf16),
        vmem((GROUP, 2, CAPACITY, feat), bf16),
        vmem((GROUP, locals_, 2, CAPACITY, feat), bf16),
        vmem((GROUP, his, CAPACITY, feat), bf16),
        vmem((GROUP, his, CAPACITY, feat), bf16),
        vmem((GROUP, his, CAPACITY, feat), bf16),
        vmem((GROUP, his, CAPACITY, feat), bf16),
        vmem((GROUP, CAPACITY, feat), f32),
        vmem((GROUP, CAPACITY, feat), bf16),
        vmem((GROUP, CAPACITY, feat), bf16),
        vmem((GROUP, 16, LANES), bf16),
        vmem((GROUP, 16, LANES), bf16),
        vmem((GROUP, 16, LANES), bf16),
        vmem((GROUP, his, 16, LANES), bf16),
        vmem((GROUP, 16, LANES), bf16),
        vmem((GROUP, 16, LANES), bf16),
        vmem((2, CAPACITY, feat), bf16),
        dma((7,)),
        dma((2,)),
        dma((2,)),
        dma((GROUP, 2)),
        dma((GROUP, 2)),
        dma((GROUP, 2, his)),
        dma((GROUP, 2, his)),
        dma((GROUP, 2, his)),
        dma((GROUP, 2, his)),
        dma((GROUP, his)),
        dma((GROUP, his)),
        dma((GROUP, his)),
        dma((GROUP, his)),
        dma((GROUP,)),
        dma((GROUP,)),
        dma((GROUP,)),
        dma((GROUP,)),
        dma((GROUP, his)),
        dma((GROUP, his)),
        dma((GROUP,)),
        dma((GROUP,)),
    ]
    in_vmem, in_hbm = pl.BlockSpec(memory_space=pltpu.VMEM), pl.BlockSpec(memory_space=pltpu.HBM)
    grads, gate_grads = pl.pallas_call(
        functools.partial(kernel, nodes, locals_),
        out_shape=(
            jax.ShapeDtypeStruct((tokens, feat), bf16),
            jax.ShapeDtypeStruct((2, tokens), f32),
        ),
        in_specs=[in_hbm] * 7,
        out_specs=(in_vmem, in_vmem),
        scratch_shapes=scratch,
        compiler_params=pltpu.CompilerParams(
            collective_id=0, has_side_effects=True, vmem_limit_bytes=48 * 1024 * 1024
        ),
        cost_estimate=pl.CostEstimate(
            flops=10 * routed * width * hidden,
            bytes_accessed=6 * width * hidden + 6 * tokens * feat,
            transcendentals=routed * hidden,
        ),
    )(layer_input, output_grad, gate_weight, up_weight, down_weight, route.T, fixed.T)
    return grads, gate_grads.T


def solution(mesh):
    in_specs = (
        P("node", "local"),
        P("node", "local"),
        P("node", None, "local"),
        P("node", None, "local"),
        P("node", "local", None),
        P("node", None),
        P("node", None),
    )
    out_specs = (P("node", "local"), P("node", None))
    run = functools.partial(body, mesh.shape["node"], mesh.shape["local"])
    return jax.shard_map(run, mesh=mesh, in_specs=in_specs, out_specs=out_specs, check_vma=False)
```

```python
import functools

import jax
import jax.numpy as jnp
from jax import lax
from jax.experimental import pallas as pl
from jax.experimental.pallas import tpu as pltpu
from jax.sharding import PartitionSpec as P

GROUP = 4
CAPACITY = 80
ORDER = (0, 3, 1, 2)
PAIR = 2
BATCHES = GROUP // PAIR
LANES = 128
MESH = pl.DeviceIdType.MESH
NT = (((1,), (1,)), ((), ()))
TN = (((0,), (0,)), ((), ()))


def dot(a, b, dims=None):
    if dims is None:
        return jnp.dot(a, b, preferred_element_type=jnp.float32)
    return lax.dot_general(a, b, dims, preferred_element_type=jnp.float32)


def split_gate(value):
    high = value.astype(jnp.bfloat16).astype(jnp.float32)
    return jnp.concatenate((high, value - high), axis=0).astype(jnp.bfloat16)


def join_gate(parts):
    parts = parts.astype(jnp.float32)
    return parts[0:8] + parts[8:16]


def lay_down(column):
    wide = jnp.broadcast_to(column, (CAPACITY, LANES))
    rest = jnp.zeros((LANES - CAPACITY, LANES), jnp.float32)
    return jnp.concatenate((wide, rest), axis=0).T[0:8]


def stand_up(row):
    return jnp.broadcast_to(row, (LANES, row.shape[1])).T


def kernel(
    nodes, locals_,
    x_hbm, g_hbm, gate_hbm, up_hbm, down_hbm, route_hbm, fixed_hbm,
    out_ref, ggrad_ref,
    x_ref, g_ref, gu, dw, route_ref, fixed_ref,
    table, packed, got, out_a, in_a, out_b, in_b, mine, out_h, in_h,
    gate_out_a, gate_in_a, gate_out_b, gate_in_b, gate_out_h, gate_in_h,
    wsem, ns, nr, hs, hr, ls, lr, sa, ra, sb, rb, sm, rm, sga, rga, sgb, rgb, sgm, rgm,
):
    tokens, feat = x_ref.shape
    hidden = dw.shape[0]
    his = locals_ // 2
    node, me = lax.axis_index("node"), lax.axis_index("local")
    hi, lo = me // 2, me % 2
    mate = hi * 2 + (1 - lo)

    def ahead(steps):
        return (lax.rem(node + steps + nodes, nodes), me)

    def beside(index):
        return (node, index)

    def turned(d):
        return lax.rem(hi + d, his)

    fetches = [
        pltpu.make_async_copy(source, dest, wsem.at[i])
        for i, (source, dest) in enumerate((
            (route_hbm, route_ref), (x_hbm, x_ref), (g_hbm, g_ref), (fixed_hbm, fixed_ref),
            (gate_hbm.at[0], gu.at[:, pl.ds(0, hidden)]),
            (up_hbm.at[0], gu.at[:, pl.ds(hidden, hidden)]),
            (down_hbm.at[0], dw),
        ))
    ]
    for copy in fetches:
        copy.start()

    barrier = pltpu.get_barrier_semaphore()
    friends = [ahead(s) for o in range(1, GROUP) for s in (o, -o)]
    friends += [beside(turned(d) * 2 + lo) for d in range(1, his)]
    friends += [beside(mate)]
    for friend in friends:
        pl.semaphore_signal(barrier, inc=1, device_id=friend, device_id_type=MESH)

    def remote(source, dest, send, recv, device):
        return pltpu.make_async_remote_copy(
            src_ref=source, dst_ref=dest, send_sem=send, recv_sem=recv,
            device_id=device, device_id_type=MESH,
        )

    def slot(o, l, k):
        return got.at[o // PAIR, l, k, pl.ds(o % PAIR * CAPACITY, CAPACITY)]

    def block_of(buffer, o, rows):
        return buffer.at[o // PAIR, pl.ds(o % PAIR * rows, rows)]

    def to_node(o, k):
        return remote(packed.at[o, k], slot(o, me, k), ns.at[o, k], nr.at[o, k], ahead(ORDER[o]))

    def to_hi(o, k, d):
        mine_ = slot(o, me, k)
        return remote(mine_, mine_, hs.at[o, k, d], hr.at[o, k, hi], beside(turned(d) * 2 + lo))

    def from_hi(o, k, d):
        h = turned(d)
        its = slot(o, h * 2 + lo, k)
        return remote(its, its, hs.at[o, k, d], hr.at[o, k, h], beside(h * 2 + lo))

    def to_mate(o, k, h):
        its = slot(o, h * 2 + lo, k)
        return remote(its, its, ls.at[o, k, h], lr.at[o, k, h], beside(mate))

    def from_mate(o, k, h):
        its = slot(o, h * 2 + 1 - lo, k)
        return remote(its, its, ls.at[o, k, h], lr.at[o, k, h], beside(mate))

    def sum_mate(b, h):
        return remote(out_a.at[b, h], in_a.at[b, h], sa.at[b, h], ra.at[b, h], beside(mate))

    def sum_hi(b, d):
        h = turned(d)
        return remote(out_b.at[b, h], in_b.at[b, hi], sb.at[b, h], rb.at[b, hi], beside(h * 2 + lo))

    def sum_from_hi(b, d):
        h = turned(d)
        return remote(out_b.at[b, h], in_b.at[b, h], sb.at[b, h], rb.at[b, h], beside(h * 2 + lo))

    def to_home(o):
        return remote(
            block_of(out_h, o, CAPACITY), block_of(in_h, o, CAPACITY),
            sm.at[o], rm.at[o], ahead(-ORDER[o]),
        )

    def gate_mate(b):
        return remote(gate_out_a.at[b], gate_in_a.at[b], sga.at[b], rga.at[b], beside(mate))

    def gate_hi(b, d):
        h = turned(d)
        return remote(
            gate_out_b.at[b], gate_in_b.at[b, hi], sgb.at[b, h], rgb.at[b, hi], beside(h * 2 + lo)
        )

    def gate_from_hi(b, d):
        h = turned(d)
        return remote(
            gate_out_b.at[b], gate_in_b.at[b, h], sgb.at[b, h], rgb.at[b, h], beside(h * 2 + lo)
        )

    def gate_home(o):
        return remote(
            block_of(gate_out_h, o, 16), block_of(gate_in_h, o, 16),
            sgm.at[o], rgm.at[o], ahead(-ORDER[o]),
        )

    fetches[0].wait()
    lanes = lax.broadcasted_iota(jnp.int32, (tokens, LANES), 1).astype(jnp.float32)
    routes = [stand_up(route_ref[k:k + 1, :].astype(jnp.float32)) for k in range(2)]
    chosen = ((routes[0] == lanes) | (routes[1] == lanes)).astype(jnp.float32)
    row = lax.broadcasted_iota(jnp.int32, (tokens, tokens), 0)
    column = lax.broadcasted_iota(jnp.int32, (tokens, tokens), 1)
    below = (column <= row).astype(jnp.float32).astype(jnp.bfloat16)
    ranks = dot(below, chosen.astype(jnp.bfloat16))
    slots = lax.broadcasted_iota(jnp.int32, (tokens, CAPACITY), 1).astype(jnp.float32) + 1.0
    tables = []
    for o in range(GROUP):
        at = slice(ORDER[o], ORDER[o] + 1)
        here = (ranks[:, at] == slots) & (chosen[:, at] > 0.5)
        tables.append(here.astype(jnp.float32).astype(jnp.bfloat16))
        table[o] = tables[o]

    def pack(o, k):
        source = x_ref if k == 0 else g_ref
        return dot(tables[o], source[...], TN).astype(jnp.bfloat16)

    fetches[1].wait()
    got[0, me, 0, pl.ds(0, CAPACITY)] = pack(0, 0)
    packed[1, 0] = pack(1, 0)
    fetches[2].wait()
    pl.semaphore_wait(barrier, len(friends))
    for d in range(1, his):
        to_hi(0, 0, d).start()
    to_node(1, 0).start()
    got[0, me, 1, pl.ds(0, CAPACITY)] = pack(0, 1)
    for d in range(1, his):
        to_hi(0, 1, d).start()
    packed[1, 1] = pack(1, 1)
    to_node(1, 1).start()
    for o in range(2, GROUP):
        for k in range(2):
            packed[o, k] = pack(o, k)
            to_node(o, k).start()
    for k in range(2):
        to_mate(0, k, hi).start()
    for copy in fetches[3:]:
        copy.wait()

    def spread(o):
        for k in range(2):
            to_node(o, k).wait_recv()
            for d in range(1, his):
                to_hi(o, k, d).start()
            to_mate(o, k, hi).start()

    def pass_on(o, k):
        for d in range(1, his):
            from_hi(o, k, d).wait_recv()
            to_mate(o, k, turned(d)).start()

    def gathered(o, k):
        for h in range(his):
            from_mate(o, k, h).wait_recv()

    def block(l):
        return pl.ds(pl.multiple_of(l * feat, 64), feat)

    def split_rows(rows):
        return jnp.concatenate([split_gate(part) for part in rows], axis=0)

    def join_rows(parts):
        return [join_gate(parts[16 * r:16 * r + 16]) for r in range(PAIR)]

    def pre(b):
        total = None
        for l in range(locals_):
            part = dot(got[b, l, 0], gu[pl.ds(l * feat, feat), :])
            total = part if total is None else total + part
        return total[:, 0:hidden], total[:, hidden:2 * hidden]

    def hidden_grad(b):
        total = None
        for l in range(locals_):
            part = dot(got[b, l, 1], dw[:, pl.ds(l * feat, feat)], NT)
            total = part if total is None else total + part
        return total

    def rest(b, pair, v):
        a, up = pair
        s = 1.0 / (1.0 + jnp.exp(-a))
        swish = a * s
        u = (v * swish).astype(jnp.bfloat16)
        w = (v * up * s * (1.0 + a * (1.0 - s))).astype(jnp.bfloat16)
        both = jnp.concatenate((w, u), axis=1)
        part = jnp.sum(swish * up * v, axis=1, keepdims=True)

        def back(l):
            return dot(both, gu[block(l), :], NT)

        def send_mate(h):
            out_a[b, h] = back(h * 2 + 1 - lo).astype(jnp.bfloat16)
            sum_mate(b, h).start()

        def with_mate(h, own):
            sum_mate(b, h).wait_recv()
            return own + in_a[b, h].astype(jnp.float32)

        for d in range(1, his):
            send_mate(turned(d))
        gate_out_a[b] = split_rows(
            [lay_down(part[CAPACITY * r:CAPACITY * (r + 1)]) for r in range(PAIR)]
        )
        gate_mate(b).start()
        parts = [back(turned(d) * 2 + lo) for d in range(1, his)]
        for d in range(1, his):
            h = turned(d)
            out_b[b, h] = with_mate(h, parts[d - 1]).astype(jnp.bfloat16)
            sum_hi(b, d).start()
        send_mate(hi)
        gate_mate(b).wait_recv()
        gate = split_rows([
            x + y for x, y in zip(join_rows(gate_out_a[b]), join_rows(gate_in_a[b]))
        ])
        gate_out_b[b] = gate
        gate_in_b[b, hi] = gate
        for d in range(1, his):
            gate_hi(b, d).start()
        mine[b] = with_mate(hi, back(me))

    def add_hi(b):
        total = mine[b]
        for d in range(1, his):
            sum_from_hi(b, d).wait_recv()
            total = total + in_b[b, turned(d)].astype(jnp.float32)
        out_h[b] = total.astype(jnp.bfloat16)
        blocks = [o for o in range(b * PAIR, (b + 1) * PAIR) if o > 0]
        for o in blocks:
            to_home(o).start()
        for d in range(1, his):
            gate_from_hi(b, d).wait_recv()
        gate = join_rows(gate_in_b[b, 0])
        for h in range(1, his):
            gate = [x + y for x, y in zip(gate, join_rows(gate_in_b[b, h]))]
        gate_out_h[b] = split_rows(gate)
        for o in blocks:
            gate_home(o).start()

    pass_on(0, 0)
    pass_on(0, 1)
    spread(1)
    pass_on(1, 0)
    for o in (0, 1):
        gathered(o, 0)
    pair = pre(0)
    pass_on(1, 1)
    for o in (0, 1):
        gathered(o, 1)
    v = hidden_grad(0)
    spread(2)
    rest(0, pair, v)
    spread(3)
    pass_on(2, 0)
    pass_on(2, 1)
    pass_on(3, 0)
    for o in (2, 3):
        gathered(o, 0)
    pair = pre(1)
    pass_on(3, 1)
    add_hi(0)
    for o in (2, 3):
        gathered(o, 1)
    v = hidden_grad(1)
    rest(1, pair, v)
    add_hi(1)

    gates = [stand_up(fixed_ref[k:k + 1, :].astype(jnp.float32)) / 65536.0 for k in range(2)]
    total = jnp.zeros((tokens, feat), jnp.float32)
    gate_total = [jnp.zeros((tokens, LANES), jnp.float32) for _ in range(2)]
    for o in range(GROUP):
        if o > 0:
            to_home(o).wait_recv()
        home = block_of(out_h if o == 0 else in_h, o, CAPACITY)
        hits = [routes[k] == float(ORDER[o]) for k in range(2)]
        weight = sum(jnp.where(hits[k], gates[k], 0.0) for k in range(2))[:, 0:1]
        total = total + weight * dot(table[o], home[...])
    for o in range(GROUP):
        if o > 0:
            gate_home(o).wait_recv()
        home = block_of(gate_out_h if o == 0 else gate_in_h, o, 16)
        pair = dot(table[o], home[...][:, 0:CAPACITY], NT)
        value = pair[:, 0:1] + pair[:, 8:9]
        for k in range(2):
            gate_total[k] = gate_total[k] + jnp.where(routes[k] == float(ORDER[o]), value, 0.0)
    out_ref[...] = total.astype(jnp.bfloat16)
    for k in range(2):
        ggrad_ref[k:k + 1, :] = gate_total[k].T[0:1]

    for o in range(GROUP):
        for k in range(2):
            for d in range(1, his):
                to_hi(o, k, d).wait_send()
            for h in range(his):
                to_mate(o, k, h).wait_send()
            if o > 0:
                to_node(o, k).wait_send()
        if o > 0:
            to_home(o).wait_send()
            gate_home(o).wait_send()
    for b in range(BATCHES):
        gate_mate(b).wait_send()
        for h in range(his):
            sum_mate(b, h).wait_send()
        for d in range(1, his):
            sum_hi(b, d).wait_send()
            gate_hi(b, d).wait_send()


def body(nodes, locals_, layer_input, output_grad, gate_weight, up_weight, down_weight, route, fixed):
    tokens, feat = layer_input.shape
    width, hidden = gate_weight.shape[1:]
    his = locals_ // 2
    bf16, f32, i32 = jnp.bfloat16, jnp.float32, jnp.int32
    vmem, dma = pltpu.VMEM, pltpu.SemaphoreType.DMA
    routed, rows = GROUP * CAPACITY, PAIR * CAPACITY
    scratch = [
        vmem((tokens, feat), bf16),
        vmem((tokens, feat), bf16),
        vmem((width, 2 * hidden), bf16),
        vmem((hidden, width), bf16),
        vmem((2, tokens), i32),
        vmem((2, tokens), i32),
        vmem((GROUP, tokens, CAPACITY), bf16),
        vmem((GROUP, 2, CAPACITY, feat), bf16),
        vmem((BATCHES, locals_, 2, rows, feat), bf16),
        vmem((BATCHES, his, rows, feat), bf16),
        vmem((BATCHES, his, rows, feat), bf16),
        vmem((BATCHES, his, rows, feat), bf16),
        vmem((BATCHES, his, rows, feat), bf16),
        vmem((BATCHES, rows, feat), f32),
        vmem((BATCHES, rows, feat), bf16),
        vmem((BATCHES, rows, feat), bf16),
        vmem((BATCHES, PAIR * 16, LANES), bf16),
        vmem((BATCHES, PAIR * 16, LANES), bf16),
        vmem((BATCHES, PAIR * 16, LANES), bf16),
        vmem((BATCHES, his, PAIR * 16, LANES), bf16),
        vmem((BATCHES, PAIR * 16, LANES), bf16),
        vmem((BATCHES, PAIR * 16, LANES), bf16),
        dma((7,)),
        dma((GROUP, 2)),
        dma((GROUP, 2)),
        dma((GROUP, 2, his)),
        dma((GROUP, 2, his)),
        dma((GROUP, 2, his)),
        dma((GROUP, 2, his)),
        dma((GROUP, his)),
        dma((GROUP, his)),
        dma((GROUP, his)),
        dma((GROUP, his)),
        dma((GROUP,)),
        dma((GROUP,)),
        dma((GROUP,)),
        dma((GROUP,)),
        dma((GROUP, his)),
        dma((GROUP, his)),
        dma((GROUP,)),
        dma((GROUP,)),
    ]
    in_vmem, anywhere = pl.BlockSpec(memory_space=pltpu.VMEM), pl.BlockSpec(memory_space=pl.ANY)
    grads, gate_grads = pl.pallas_call(
        functools.partial(kernel, nodes, locals_),
        out_shape=(
            jax.ShapeDtypeStruct((tokens, feat), bf16),
            jax.ShapeDtypeStruct((2, tokens), f32),
        ),
        in_specs=[anywhere] * 7,
        out_specs=(in_vmem, in_vmem),
        scratch_shapes=scratch,
        compiler_params=pltpu.CompilerParams(
            collective_id=0, has_side_effects=True, vmem_limit_bytes=60 * 1024 * 1024
        ),
        cost_estimate=pl.CostEstimate(
            flops=10 * routed * width * hidden,
            bytes_accessed=6 * width * hidden + 6 * tokens * feat,
            transcendentals=routed * hidden,
        ),
    )(layer_input, output_grad, gate_weight, up_weight, down_weight, route.T, fixed.T)
    return grads, gate_grads.T


def solution(mesh):
    in_specs = (
        P("node", "local"),
        P("node", "local"),
        P("node", None, "local"),
        P("node", None, "local"),
        P("node", "local", None),
        P("node", None),
        P("node", None),
    )
    out_specs = (P("node", "local"), P("node", None))
    run = functools.partial(body, mesh.shape["node"], mesh.shape["local"])
    return jax.shard_map(run, mesh=mesh, in_specs=in_specs, out_specs=out_specs, check_vma=False)
```

```python
import functools

import jax
import jax.numpy as jnp
from jax import lax
from jax.experimental import pallas as pl
from jax.experimental.pallas import tpu as pltpu
from jax.sharding import PartitionSpec as P

GROUP = 4
CAPACITY = 80
LANES = 128
MESH = pl.DeviceIdType.MESH
NT = (((1,), (1,)), ((), ()))
TN = (((0,), (0,)), ((), ()))


def dot(a, b, dims=None):
    if dims is None:
        return jnp.dot(a, b, preferred_element_type=jnp.float32)
    return lax.dot_general(a, b, dims, preferred_element_type=jnp.float32)


def split_gate(value):
    high = value.astype(jnp.bfloat16).astype(jnp.float32)
    return jnp.concatenate((high, value - high), axis=0).astype(jnp.bfloat16)


def join_gate(parts):
    parts = parts.astype(jnp.float32)
    return parts[0:8] + parts[8:16]


def lay_down(column):
    wide = jnp.broadcast_to(column, (CAPACITY, LANES))
    rest = jnp.zeros((LANES - CAPACITY, LANES), jnp.float32)
    return jnp.concatenate((wide, rest), axis=0).T[0:8]


def stand_up(row):
    return jnp.broadcast_to(row, (LANES, row.shape[1])).T


def kernel(
    nodes, locals_,
    x_hbm, g_hbm, gate_hbm, up_hbm, down_hbm, route_hbm, fixed_hbm,
    out_ref, ggrad_ref,
    x_ref, g_ref, gu, dw, route_ref, fixed_ref,
    table, packed, got, out_a, in_a, out_b, in_b, mine, out_h, in_h,
    gate_out_a, gate_in_a, gate_out_b, gate_in_b, gate_out_h, gate_in_h,
    wsem, ns, nr, hs, hr, ls, lr, sa, ra, sb, rb, sm, rm, sga, rga, sgb, rgb, sgm, rgm,
):
    tokens, feat = x_ref.shape
    hidden = dw.shape[0]
    his = locals_ // 2
    node, me = lax.axis_index("node"), lax.axis_index("local")
    hi, lo = me // 2, me % 2
    mate = hi * 2 + (1 - lo)

    def ahead(steps):
        return (lax.rem(node + steps + nodes, nodes), me)

    def beside(index):
        return (node, index)

    def turned(d):
        return lax.rem(hi + d, his)

    fetches = [
        pltpu.make_async_copy(source, dest, wsem.at[i])
        for i, (source, dest) in enumerate((
            (route_hbm, route_ref), (x_hbm, x_ref), (g_hbm, g_ref), (fixed_hbm, fixed_ref),
            (gate_hbm.at[0], gu.at[:, pl.ds(0, hidden)]),
            (up_hbm.at[0], gu.at[:, pl.ds(hidden, hidden)]),
            (down_hbm.at[0], dw),
        ))
    ]
    for copy in fetches[:4]:
        copy.start()

    barrier = pltpu.get_barrier_semaphore()
    friends = [ahead(s) for o in range(1, GROUP) for s in (o, -o)]
    friends += [beside(turned(d) * 2 + lo) for d in range(1, his)]
    friends += [beside(mate)]
    for friend in friends:
        pl.semaphore_signal(barrier, inc=1, device_id=friend, device_id_type=MESH)

    def remote(source, dest, send, recv, device):
        return pltpu.make_async_remote_copy(
            src_ref=source, dst_ref=dest, send_sem=send, recv_sem=recv,
            device_id=device, device_id_type=MESH,
        )

    def to_node(o, k):
        return remote(packed.at[o, k], got.at[o, me, k], ns.at[o, k], nr.at[o, k], ahead(o))

    def to_hi(o, k, d):
        return remote(
            got.at[o, me, k], got.at[o, me, k], hs.at[o, k, d], hr.at[o, k, hi],
            beside(turned(d) * 2 + lo),
        )

    def from_hi(o, k, d):
        h = turned(d)
        slot = got.at[o, h * 2 + lo, k]
        return remote(slot, slot, hs.at[o, k, d], hr.at[o, k, h], beside(h * 2 + lo))

    def to_mate(o, k, h):
        slot = got.at[o, h * 2 + lo, k]
        return remote(slot, slot, ls.at[o, k, h], lr.at[o, k, h], beside(mate))

    def from_mate(o, k, h):
        slot = got.at[o, h * 2 + 1 - lo, k]
        return remote(slot, slot, ls.at[o, k, h], lr.at[o, k, h], beside(mate))

    def sum_mate(o, h):
        return remote(out_a.at[o, h], in_a.at[o, h], sa.at[o, h], ra.at[o, h], beside(mate))

    def sum_hi(o, d):
        h = turned(d)
        return remote(out_b.at[o, h], in_b.at[o, hi], sb.at[o, h], rb.at[o, hi], beside(h * 2 + lo))

    def sum_from_hi(o, d):
        h = turned(d)
        return remote(out_b.at[o, h], in_b.at[o, h], sb.at[o, h], rb.at[o, h], beside(h * 2 + lo))

    def to_home(o):
        return remote(out_h.at[o], in_h.at[o], sm.at[o], rm.at[o], ahead(-o))

    def gate_mate(o):
        return remote(gate_out_a.at[o], gate_in_a.at[o], sga.at[o], rga.at[o], beside(mate))

    def gate_hi(o, d):
        h = turned(d)
        return remote(
            gate_out_b.at[o], gate_in_b.at[o, hi], sgb.at[o, h], rgb.at[o, hi], beside(h * 2 + lo)
        )

    def gate_from_hi(o, d):
        h = turned(d)
        return remote(
            gate_out_b.at[o], gate_in_b.at[o, h], sgb.at[o, h], rgb.at[o, h], beside(h * 2 + lo)
        )

    def gate_home(o):
        return remote(gate_out_h.at[o], gate_in_h.at[o], sgm.at[o], rgm.at[o], ahead(-o))

    fetches[0].wait()
    lanes = lax.broadcasted_iota(jnp.int32, (tokens, LANES), 1).astype(jnp.float32)
    routes = [stand_up(route_ref[k:k + 1, :].astype(jnp.float32)) for k in range(2)]
    chosen = ((routes[0] == lanes) | (routes[1] == lanes)).astype(jnp.float32)
    row = lax.broadcasted_iota(jnp.int32, (tokens, tokens), 0)
    column = lax.broadcasted_iota(jnp.int32, (tokens, tokens), 1)
    below = (column <= row).astype(jnp.float32).astype(jnp.bfloat16)
    ranks = dot(below, chosen.astype(jnp.bfloat16))
    slots = lax.broadcasted_iota(jnp.int32, (tokens, CAPACITY), 1).astype(jnp.float32) + 1.0
    tables = []
    for o in range(GROUP):
        here = (ranks[:, o:o + 1] == slots) & (chosen[:, o:o + 1] > 0.5)
        tables.append(here.astype(jnp.float32).astype(jnp.bfloat16))
        table[o] = tables[o]

    def pack(o, k):
        source = x_ref if k == 0 else g_ref
        return dot(tables[o], source[...], TN).astype(jnp.bfloat16)

    fetches[1].wait()
    got[0, me, 0] = pack(0, 0)
    packed[1, 0] = pack(1, 0)
    fetches[2].wait()
    pl.semaphore_wait(barrier, len(friends))
    for d in range(1, his):
        to_hi(0, 0, d).start()
    to_node(1, 0).start()
    got[0, me, 1] = pack(0, 1)
    for d in range(1, his):
        to_hi(0, 1, d).start()
    packed[1, 1] = pack(1, 1)
    to_node(1, 1).start()
    for o in range(2, GROUP):
        for k in range(2):
            packed[o, k] = pack(o, k)
            to_node(o, k).start()
    for copy in fetches[4:]:
        copy.start()
    for k in range(2):
        to_mate(0, k, hi).start()
    for copy in fetches[3:]:
        copy.wait()

    def spread(o):
        for k in range(2):
            to_node(o, k).wait_recv()
            for d in range(1, his):
                to_hi(o, k, d).start()
            to_mate(o, k, hi).start()

    def block(l):
        return pl.ds(pl.multiple_of(l * feat, 64), feat)

    def pass_on(o, k):
        for d in range(1, his):
            from_hi(o, k, d).wait_recv()
            to_mate(o, k, turned(d)).start()

    def gathered(o, k):
        for h in range(his):
            from_mate(o, k, h).wait_recv()

    def compute(o):
        pass_on(o, 0)

        @pl.when(o >= 1)
        def _():
            add_hi(o - 1)

        gathered(o, 0)
        both = jnp.zeros((CAPACITY, 2 * hidden), jnp.float32)
        for l in range(locals_):
            both = both + dot(got[o, l, 0], gu[pl.ds(l * feat, feat), :])
        pass_on(o, 1)
        gathered(o, 1)
        v = jnp.zeros((CAPACITY, hidden), jnp.float32)
        for l in range(locals_):
            v = v + dot(got[o, l, 1], dw[:, pl.ds(l * feat, feat)], NT)
        a, b = both[:, 0:hidden], both[:, hidden:2 * hidden]
        s = 1.0 / (1.0 + jnp.exp(-a))
        swish = a * s
        u = (v * swish).astype(jnp.bfloat16)
        w = (v * b * s * (1.0 + a * (1.0 - s))).astype(jnp.bfloat16)
        grads = jnp.concatenate((w, u), axis=1)
        gate_out_a[o] = split_gate(lay_down(jnp.sum(swish * b * v, axis=1, keepdims=True)))
        gate_mate(o).start()

        def back(l):
            return dot(grads, gu[block(l), :], NT)

        def send_mate(h):
            out_a[o, h] = back(h * 2 + 1 - lo).astype(jnp.bfloat16)
            sum_mate(o, h).start()

        def with_mate(h, part):
            sum_mate(o, h).wait_recv()
            return part + in_a[o, h].astype(jnp.float32)

        for d in range(1, his):
            send_mate(turned(d))
        parts = [back(turned(d) * 2 + lo) for d in range(1, his)]
        send_mate(hi)
        for d in range(1, his):
            h = turned(d)
            out_b[o, h] = with_mate(h, parts[d - 1]).astype(jnp.bfloat16)
            sum_hi(o, d).start()
        gate_mate(o).wait_recv()
        gate = split_gate(join_gate(gate_out_a[o]) + join_gate(gate_in_a[o]))
        gate_out_b[o] = gate
        gate_in_b[o, hi] = gate
        for d in range(1, his):
            gate_hi(o, d).start()
        mine[o] = with_mate(hi, back(me))

    def add_hi(o):
        total = mine[o]
        for d in range(1, his):
            sum_from_hi(o, d).wait_recv()
            total = total + in_b[o, turned(d)].astype(jnp.float32)
        out_h[o] = total.astype(jnp.bfloat16)

        @pl.when(o > 0)
        def _():
            to_home(o).start()

        for d in range(1, his):
            gate_from_hi(o, d).wait_recv()
        gate = join_gate(gate_in_b[o, 0])
        for h in range(1, his):
            gate = gate + join_gate(gate_in_b[o, h])
        gate_out_h[o] = split_gate(gate)

        @pl.when(o > 0)
        def _():
            gate_home(o).start()

    def step(i, carry):
        @pl.when(i + 1 < GROUP)
        def _():
            spread(i + 1)

        compute(i)
        return carry

    lax.fori_loop(0, GROUP, step, 0)
    add_hi(GROUP - 1)

    gates = [stand_up(fixed_ref[k:k + 1, :].astype(jnp.float32)) / 65536.0 for k in range(2)]
    total = jnp.zeros((tokens, feat), jnp.float32)
    gate_total = [jnp.zeros((tokens, LANES), jnp.float32) for _ in range(2)]
    for o in range(GROUP):
        if o > 0:
            to_home(o).wait_recv()
        home = out_h if o == 0 else in_h
        hits = [routes[k] == float(o) for k in range(2)]
        weight = sum(jnp.where(hits[k], gates[k], 0.0) for k in range(2))[:, 0:1]
        total = total + weight * dot(table[o], home[o])
    for o in range(GROUP):
        if o > 0:
            gate_home(o).wait_recv()
        home = gate_out_h if o == 0 else gate_in_h
        pair = dot(table[o], home[o][:, 0:CAPACITY], NT)
        value = pair[:, 0:1] + pair[:, 8:9]
        for k in range(2):
            gate_total[k] = gate_total[k] + jnp.where(routes[k] == float(o), value, 0.0)
    out_ref[...] = total.astype(jnp.bfloat16)
    for k in range(2):
        ggrad_ref[k:k + 1, :] = gate_total[k].T[0:1]

    def finish(o, carry):
        for k in range(2):
            for d in range(1, his):
                to_hi(o, k, d).wait_send()
            for h in range(his):
                to_mate(o, k, h).wait_send()
        gate_mate(o).wait_send()
        for h in range(his):
            sum_mate(o, h).wait_send()
        for d in range(1, his):
            sum_hi(o, d).wait_send()
            gate_hi(o, d).wait_send()

        @pl.when(o > 0)
        def _():
            for k in range(2):
                to_node(o, k).wait_send()
            to_home(o).wait_send()
            gate_home(o).wait_send()

        return carry

    lax.fori_loop(0, GROUP, finish, 0)


def body(nodes, locals_, layer_input, output_grad, gate_weight, up_weight, down_weight, route, fixed):
    tokens, feat = layer_input.shape
    width, hidden = gate_weight.shape[1:]
    his = locals_ // 2
    bf16, f32, i32 = jnp.bfloat16, jnp.float32, jnp.int32
    vmem, dma = pltpu.VMEM, pltpu.SemaphoreType.DMA
    routed = GROUP * CAPACITY
    scratch = [
        vmem((tokens, feat), bf16),
        vmem((tokens, feat), bf16),
        vmem((width, 2 * hidden), bf16),
        vmem((hidden, width), bf16),
        vmem((2, tokens), i32),
        vmem((2, tokens), i32),
        vmem((GROUP, tokens, CAPACITY), bf16),
        vmem((GROUP, 2, CAPACITY, feat), bf16),
        vmem((GROUP, locals_, 2, CAPACITY, feat), bf16),
        vmem((GROUP, his, CAPACITY, feat), bf16),
        vmem((GROUP, his, CAPACITY, feat), bf16),
        vmem((GROUP, his, CAPACITY, feat), bf16),
        vmem((GROUP, his, CAPACITY, feat), bf16),
        vmem((GROUP, CAPACITY, feat), f32),
        vmem((GROUP, CAPACITY, feat), bf16),
        vmem((GROUP, CAPACITY, feat), bf16),
        vmem((GROUP, 16, LANES), bf16),
        vmem((GROUP, 16, LANES), bf16),
        vmem((GROUP, 16, LANES), bf16),
        vmem((GROUP, his, 16, LANES), bf16),
        vmem((GROUP, 16, LANES), bf16),
        vmem((GROUP, 16, LANES), bf16),
        dma((7,)),
        dma((GROUP, 2)),
        dma((GROUP, 2)),
        dma((GROUP, 2, his)),
        dma((GROUP, 2, his)),
        dma((GROUP, 2, his)),
        dma((GROUP, 2, his)),
        dma((GROUP, his)),
        dma((GROUP, his)),
        dma((GROUP, his)),
        dma((GROUP, his)),
        dma((GROUP,)),
        dma((GROUP,)),
        dma((GROUP,)),
        dma((GROUP,)),
        dma((GROUP, his)),
        dma((GROUP, his)),
        dma((GROUP,)),
        dma((GROUP,)),
    ]
    in_vmem, anywhere = pl.BlockSpec(memory_space=pltpu.VMEM), pl.BlockSpec(memory_space=pl.ANY)
    grads, gate_grads = pl.pallas_call(
        functools.partial(kernel, nodes, locals_),
        out_shape=(
            jax.ShapeDtypeStruct((tokens, feat), bf16),
            jax.ShapeDtypeStruct((2, tokens), f32),
        ),
        in_specs=[anywhere] * 7,
        out_specs=(in_vmem, in_vmem),
        scratch_shapes=scratch,
        compiler_params=pltpu.CompilerParams(
            collective_id=0, has_side_effects=True, vmem_limit_bytes=60 * 1024 * 1024
        ),
        cost_estimate=pl.CostEstimate(
            flops=10 * routed * width * hidden,
            bytes_accessed=6 * width * hidden + 6 * tokens * feat,
            transcendentals=routed * hidden,
        ),
    )(layer_input, output_grad, gate_weight, up_weight, down_weight, route.T, fixed.T)
    return grads, gate_grads.T


def solution(mesh):
    in_specs = (
        P("node", "local"),
        P("node", "local"),
        P("node", None, "local"),
        P("node", None, "local"),
        P("node", "local", None),
        P("node", None),
        P("node", None),
    )
    out_specs = (P("node", "local"), P("node", None))
    run = functools.partial(body, mesh.shape["node"], mesh.shape["local"])
    return jax.shard_map(run, mesh=mesh, in_specs=in_specs, out_specs=out_specs, check_vma=False)
```

```python
import functools

import jax
import jax.numpy as jnp
from jax import lax
from jax.experimental import pallas as pl
from jax.experimental.pallas import tpu as pltpu
from jax.sharding import PartitionSpec as P

GROUP = 4
CAPACITY = 80
LANES = 128
MESH = pl.DeviceIdType.MESH
NT = (((1,), (1,)), ((), ()))
TN = (((0,), (0,)), ((), ()))


def dot(a, b, dims=None):
    if dims is None:
        return jnp.dot(a, b, preferred_element_type=jnp.float32)
    return lax.dot_general(a, b, dims, preferred_element_type=jnp.float32)


def lane_index(rows):
    return lax.broadcasted_iota(jnp.int32, (rows, LANES), 1)


def split_gate(value):
    high = value.astype(jnp.bfloat16).astype(jnp.float32)
    low = value - high
    return jnp.where(lane_index(value.shape[0]) < LANES // 2, high, low).astype(jnp.bfloat16)


def join_gate(parts):
    lanes = lane_index(parts.shape[0])
    keep = (lanes == 0) | (lanes == LANES // 2)
    return jnp.sum(jnp.where(keep, parts.astype(jnp.float32), 0.0), axis=1, keepdims=True)


def stand_up(row):
    return jnp.broadcast_to(row, (LANES, row.shape[1])).T


def kernel(
    nodes, locals_,
    x_hbm, g_hbm, gate_hbm, up_hbm, down_hbm, route_hbm, fixed_hbm,
    out_ref, ggrad_ref,
    x_ref, g_ref, route_ref, fixed_ref, gw, uw, dw, table, packed, got, out_a, in_a, own, own_gate, out_b, in_b, mine, out_h, in_h,
    wsem, ns, nr, hs, hr, ls, lr, sa, ra, sb, rb, sm, rm,
):
    tokens, feat = x_ref.shape
    wide = out_h.shape[2]
    gate_lanes = pl.ds(wide - LANES, LANES)
    his = locals_ // 2
    node, me = lax.axis_index("node"), lax.axis_index("local")
    hi, lo = me // 2, me % 2
    mate = hi * 2 + (1 - lo)

    def ahead(steps):
        return (lax.rem(node + steps + nodes, nodes), me)

    def beside(index):
        return (node, index)

    def turned(d):
        return lax.rem(hi + d, his)

    fetches = [
        pltpu.make_async_copy(source, dest, wsem.at[i])
        for i, (source, dest) in enumerate((
            (route_hbm, route_ref), (x_hbm, x_ref), (g_hbm, g_ref), (fixed_hbm, fixed_ref),
            (gate_hbm.at[0], gw), (up_hbm.at[0], uw), (down_hbm.at[0], dw),
        ))
    ]
    for copy in fetches:
        copy.start()

    barrier = pltpu.get_barrier_semaphore()
    friends = [ahead(s) for o in range(1, GROUP) for s in (o, -o)]
    friends += [beside(turned(d) * 2 + lo) for d in range(1, his)]
    friends += [beside(mate)]
    for friend in friends:
        pl.semaphore_signal(barrier, inc=1, device_id=friend, device_id_type=MESH)

    def remote(source, dest, send, recv, device):
        return pltpu.make_async_remote_copy(
            src_ref=source, dst_ref=dest, send_sem=send, recv_sem=recv,
            device_id=device, device_id_type=MESH,
        )

    def to_node(o, k):
        return remote(packed.at[o, k], got.at[o, me, k], ns.at[o, k], nr.at[o, k], ahead(o))

    def to_hi(o, k, d):
        return remote(
            got.at[o, me, k], got.at[o, me, k], hs.at[o, k, d], hr.at[o, k, hi],
            beside(turned(d) * 2 + lo),
        )

    def from_hi(o, k, d):
        h = turned(d)
        slot = got.at[o, h * 2 + lo, k]
        return remote(slot, slot, hs.at[o, k, d], hr.at[o, k, h], beside(h * 2 + lo))

    def to_mate(o, k, h):
        slot = got.at[o, h * 2 + lo, k]
        return remote(slot, slot, ls.at[o, k, h], lr.at[o, k, h], beside(mate))

    def from_mate(o, k, h):
        slot = got.at[o, h * 2 + 1 - lo, k]
        return remote(slot, slot, ls.at[o, k, h], lr.at[o, k, h], beside(mate))

    def sum_mate(o):
        return remote(out_a.at[o], in_a.at[o], sa.at[o], ra.at[o], beside(mate))

    def sum_hi(o, d):
        h = turned(d)
        return remote(out_b.at[o, h], in_b.at[o, hi], sb.at[o, h], rb.at[o, hi], beside(h * 2 + lo))

    def sum_from_hi(o, d):
        h = turned(d)
        return remote(out_b.at[o, h], in_b.at[o, h], sb.at[o, h], rb.at[o, h], beside(h * 2 + lo))

    def to_home(o):
        return remote(out_h.at[o], in_h.at[o], sm.at[o], rm.at[o], ahead(-o))

    fetches[0].wait()
    lanes = lane_index(tokens).astype(jnp.float32)
    routes = [stand_up(route_ref[k:k + 1, :].astype(jnp.float32)) for k in range(2)]
    chosen = ((routes[0] == lanes) | (routes[1] == lanes)).astype(jnp.float32)
    row = lax.broadcasted_iota(jnp.int32, (tokens, tokens), 0)
    column = lax.broadcasted_iota(jnp.int32, (tokens, tokens), 1)
    below = (column <= row).astype(jnp.float32).astype(jnp.bfloat16)
    ranks = dot(below, chosen.astype(jnp.bfloat16))
    slots = lax.broadcasted_iota(jnp.int32, (tokens, CAPACITY), 1).astype(jnp.float32) + 1.0
    tables = []
    for o in range(GROUP):
        here = (ranks[:, o:o + 1] == slots) & (chosen[:, o:o + 1] > 0.5)
        tables.append(here.astype(jnp.float32).astype(jnp.bfloat16))
        table[o] = tables[o]

    def pack(o, k):
        source = x_ref if k == 0 else g_ref
        return dot(tables[o], source[...], TN).astype(jnp.bfloat16)

    for k in range(2):
        fetches[1 + k].wait()
        got[0, me, k] = pack(0, k)
    pl.semaphore_wait(barrier, len(friends))
    for k in range(2):
        for d in range(1, his):
            to_hi(0, k, d).start()
    for o in range(1, GROUP):
        for k in range(2):
            packed[o, k] = pack(o, k)
            to_node(o, k).start()
    for k in range(2):
        to_mate(0, k, hi).start()
    for copy in fetches[3:]:
        copy.wait()

    def spread(o):
        for k in range(2):
            to_node(o, k).wait_recv()
            for d in range(1, his):
                to_hi(o, k, d).start()
            to_mate(o, k, hi).start()

    def pass_on(o):
        for k in range(2):
            for d in range(1, his):
                from_hi(o, k, d).wait_recv()
                to_mate(o, k, turned(d)).start()

    def compute(o):
        for k in range(2):
            for h in range(his):
                from_mate(o, k, h).wait_recv()
        a = b = v = None
        for l in range(locals_):
            rows = pl.ds(l * feat, feat)
            x, g = got[o, l, 0], got[o, l, 1]
            pa, pb, pv = dot(x, gw[rows, :]), dot(x, uw[rows, :]), dot(g, dw[:, rows], NT)
            a, b, v = (pa, pb, pv) if a is None else (a + pa, b + pb, v + pv)
        s = 1.0 / (1.0 + jnp.exp(-a))
        swish = a * s
        part = split_gate(jnp.sum(swish * b * v, axis=1, keepdims=True))
        u = (v * swish).astype(jnp.bfloat16)
        w = (v * b * s * (1.0 + a * (1.0 - s))).astype(jnp.bfloat16)

        def back(l):
            rows = pl.ds(pl.multiple_of(l * feat, 64), feat)
            return dot(w, gw[rows, :], NT) + dot(u, uw[rows, :], NT)

        for h in range(his):
            out_a[o, h, :, pl.ds(0, feat)] = back(h * 2 + 1 - lo).astype(jnp.bfloat16)
            out_a[o, h, :, gate_lanes] = part
        sum_mate(o).start()
        own_gate[...] = part
        for h in range(his):
            own[h] = back(h * 2 + lo)

    def add_mate(o):
        sum_mate(o).wait_recv()
        gate = split_gate(join_gate(own_gate[...]) + join_gate(in_a[o, 0, :, gate_lanes]))
        for d in range(1, his):
            h = turned(d)
            total = own[h] + in_a[o, h, :, pl.ds(0, feat)].astype(jnp.float32)
            out_b[o, h, :, pl.ds(0, feat)] = total.astype(jnp.bfloat16)
            out_b[o, h, :, gate_lanes] = gate
            sum_hi(o, d).start()
        mine[o] = own[hi] + in_a[o, hi, :, pl.ds(0, feat)].astype(jnp.float32)
        in_b[o, hi, :, gate_lanes] = gate

    def add_hi(o):
        total = mine[o]
        for d in range(1, his):
            sum_from_hi(o, d).wait_recv()
            total = total + in_b[o, turned(d), :, pl.ds(0, feat)].astype(jnp.float32)
        gate = join_gate(in_b[o, 0, :, gate_lanes])
        for h in range(1, his):
            gate = gate + join_gate(in_b[o, h, :, gate_lanes])
        out_h[o, :, pl.ds(0, feat)] = total.astype(jnp.bfloat16)
        out_h[o, :, gate_lanes] = split_gate(gate)

        @pl.when(o > 0)
        def _():
            to_home(o).start()

    def step(i, carry):
        @pl.when(i >= 1)
        def _():
            add_mate(i - 1)

        @pl.when(i + 1 < GROUP)
        def _():
            spread(i + 1)

        @pl.when(i < GROUP)
        def _():
            pass_on(i)

        @pl.when(i >= 1)
        def _():
            add_hi(i - 1)

        @pl.when(i < GROUP)
        def _():
            compute(i)

        return carry

    lax.fori_loop(0, GROUP + 1, step, 0)

    gates = [stand_up(fixed_ref[k:k + 1, :].astype(jnp.float32)) / 65536.0 for k in range(2)]
    total = jnp.zeros((tokens, feat), jnp.float32)
    gate_total = [jnp.zeros((tokens, LANES), jnp.float32) for _ in range(2)]
    for o in range(GROUP):
        if o > 0:
            to_home(o).wait_recv()
        home = out_h if o == 0 else in_h
        hits = [routes[k] == float(o) for k in range(2)]
        weight = sum(jnp.where(hits[k], gates[k], 0.0) for k in range(2))[:, 0:1]
        total = total + weight * dot(table[o], home[o, :, pl.ds(0, feat)])
        back_gate = join_gate(dot(table[o], home[o, :, gate_lanes]))
        for k in range(2):
            gate_total[k] = gate_total[k] + jnp.where(hits[k], back_gate, 0.0)
    out_ref[...] = total.astype(jnp.bfloat16)
    for k in range(2):
        ggrad_ref[k:k + 1, :] = gate_total[k].T[0:1]

    def finish(o, carry):
        for k in range(2):
            for d in range(1, his):
                to_hi(o, k, d).wait_send()
            for h in range(his):
                to_mate(o, k, h).wait_send()
        sum_mate(o).wait_send()
        for d in range(1, his):
            sum_hi(o, d).wait_send()

        @pl.when(o > 0)
        def _():
            for k in range(2):
                to_node(o, k).wait_send()
            to_home(o).wait_send()

        return carry

    lax.fori_loop(0, GROUP, finish, 0)


def body(nodes, locals_, layer_input, output_grad, gate_weight, up_weight, down_weight, route, fixed):
    tokens, feat = layer_input.shape
    width, hidden = gate_weight.shape[1:]
    his = locals_ // 2
    wide = -(-feat // LANES) * LANES + LANES
    bf16, f32 = jnp.bfloat16, jnp.float32
    vmem, dma = pltpu.VMEM, pltpu.SemaphoreType.DMA
    scratch = [
        vmem((tokens, feat), bf16),
        vmem((tokens, feat), bf16),
        vmem((2, tokens), jnp.int32),
        vmem((2, tokens), jnp.int32),
        vmem((width, hidden), bf16),
        vmem((width, hidden), bf16),
        vmem((hidden, width), bf16),
        vmem((GROUP, tokens, CAPACITY), bf16),
        vmem((GROUP, 2, CAPACITY, feat), bf16),
        vmem((GROUP, locals_, 2, CAPACITY, feat), bf16),
        vmem((GROUP, his, CAPACITY, wide), bf16),
        vmem((GROUP, his, CAPACITY, wide), bf16),
        vmem((his, CAPACITY, feat), f32),
        vmem((CAPACITY, LANES), bf16),
        vmem((GROUP, his, CAPACITY, wide), bf16),
        vmem((GROUP, his, CAPACITY, wide), bf16),
        vmem((GROUP, CAPACITY, feat), f32),
        vmem((GROUP, CAPACITY, wide), bf16),
        vmem((GROUP, CAPACITY, wide), bf16),
        dma((7,)),
        dma((GROUP, 2)),
        dma((GROUP, 2)),
        dma((GROUP, 2, his)),
        dma((GROUP, 2, his)),
        dma((GROUP, 2, his)),
        dma((GROUP, 2, his)),
        dma((GROUP,)),
        dma((GROUP,)),
        dma((GROUP, his)),
        dma((GROUP, his)),
        dma((GROUP,)),
        dma((GROUP,)),
    ]
    in_vmem, anywhere = pl.BlockSpec(memory_space=pltpu.VMEM), pl.BlockSpec(memory_space=pl.ANY)
    routed = GROUP * CAPACITY
    grads, gate_grads = pl.pallas_call(
        functools.partial(kernel, nodes, locals_),
        out_shape=(
            jax.ShapeDtypeStruct((tokens, feat), bf16),
            jax.ShapeDtypeStruct((2, tokens), f32),
        ),
        in_specs=[anywhere] * 7,
        out_specs=(in_vmem, in_vmem),
        scratch_shapes=scratch,
        compiler_params=pltpu.CompilerParams(
            collective_id=0, has_side_effects=True, vmem_limit_bytes=60 * 1024 * 1024
        ),
        cost_estimate=pl.CostEstimate(
            flops=10 * routed * width * hidden,
            bytes_accessed=6 * width * hidden + 6 * tokens * feat,
            transcendentals=routed * hidden,
        ),
    )(layer_input, output_grad, gate_weight, up_weight, down_weight, route.T, fixed.T)
    return grads, gate_grads.T


def solution(mesh):
    in_specs = (
        P("node", "local"),
        P("node", "local"),
        P("node", None, "local"),
        P("node", None, "local"),
        P("node", "local", None),
        P("node", None),
        P("node", None),
    )
    out_specs = (P("node", "local"), P("node", None))
    run = functools.partial(body, mesh.shape["node"], mesh.shape["local"])
    return jax.shard_map(run, mesh=mesh, in_specs=in_specs, out_specs=out_specs, check_vma=False)
```

```python
import functools

import jax
import jax.numpy as jnp
from jax import lax
from jax.experimental import pallas as pl
from jax.experimental.pallas import tpu as pltpu
from jax.sharding import PartitionSpec as P

GROUP = 4
CAPACITY = 80
LANES = 128
MESH = pl.DeviceIdType.MESH
NT = (((1,), (1,)), ((), ()))
TN = (((0,), (0,)), ((), ()))


def dot(a, b, dims=None):
    if dims is None:
        return jnp.dot(a, b, preferred_element_type=jnp.float32)
    return lax.dot_general(a, b, dims, preferred_element_type=jnp.float32)


def lane_index(rows):
    return lax.broadcasted_iota(jnp.int32, (rows, LANES), 1)


def split_gate(value):
    high = value.astype(jnp.bfloat16).astype(jnp.float32)
    low = value - high
    return jnp.where(lane_index(value.shape[0]) < LANES // 2, high, low).astype(jnp.bfloat16)


def join_gate(parts):
    lanes = lane_index(parts.shape[0])
    keep = (lanes == 0) | (lanes == LANES // 2)
    return jnp.sum(jnp.where(keep, parts.astype(jnp.float32), 0.0), axis=1, keepdims=True)


def stand_up(row):
    return jnp.broadcast_to(row, (LANES, row.shape[1])).T


def kernel(
    nodes, locals_,
    x_hbm, g_hbm, gate_hbm, up_hbm, down_hbm, route_hbm, fixed_hbm,
    out_ref, ggrad_ref,
    x_ref, g_ref, route_ref, fixed_ref, gw, uw, dw, table, packed, got, out_a, in_a, own, own_gate, out_b, in_b, mine, out_h, in_h,
    wsem, ns, nr, hs, hr, ls, lr, sa, ra, sb, rb, sm, rm,
):
    tokens, feat = x_ref.shape
    wide = out_h.shape[2]
    gate_lanes = pl.ds(wide - LANES, LANES)
    his = locals_ // 2
    node, me = lax.axis_index("node"), lax.axis_index("local")
    hi, lo = me // 2, me % 2
    mate = hi * 2 + (1 - lo)

    def ahead(steps):
        return (lax.rem(node + steps + nodes, nodes), me)

    def beside(index):
        return (node, index)

    def turned(d):
        return lax.rem(hi + d, his)

    fetches = [
        pltpu.make_async_copy(source, dest, wsem.at[i])
        for i, (source, dest) in enumerate((
            (route_hbm, route_ref), (x_hbm, x_ref), (g_hbm, g_ref), (fixed_hbm, fixed_ref),
            (gate_hbm.at[0], gw), (up_hbm.at[0], uw), (down_hbm.at[0], dw),
        ))
    ]
    for copy in fetches:
        copy.start()

    barrier = pltpu.get_barrier_semaphore()
    friends = [ahead(s) for o in range(1, GROUP) for s in (o, -o)]
    friends += [beside(turned(d) * 2 + lo) for d in range(1, his)]
    friends += [beside(mate)]
    for friend in friends:
        pl.semaphore_signal(barrier, inc=1, device_id=friend, device_id_type=MESH)

    def remote(source, dest, send, recv, device):
        return pltpu.make_async_remote_copy(
            src_ref=source, dst_ref=dest, send_sem=send, recv_sem=recv,
            device_id=device, device_id_type=MESH,
        )

    def to_node(o, k):
        return remote(packed.at[o, k], got.at[o, me, k], ns.at[o, k], nr.at[o, k], ahead(o))

    def to_hi(o, k, d):
        return remote(
            got.at[o, me, k], got.at[o, me, k], hs.at[o, k, d], hr.at[o, k, hi],
            beside(turned(d) * 2 + lo),
        )

    def from_hi(o, k, d):
        h = turned(d)
        slot = got.at[o, h * 2 + lo, k]
        return remote(slot, slot, hs.at[o, k, d], hr.at[o, k, h], beside(h * 2 + lo))

    def to_mate(o, k, h):
        slot = got.at[o, h * 2 + lo, k]
        return remote(slot, slot, ls.at[o, k, h], lr.at[o, k, h], beside(mate))

    def from_mate(o, k, h):
        slot = got.at[o, h * 2 + 1 - lo, k]
        return remote(slot, slot, ls.at[o, k, h], lr.at[o, k, h], beside(mate))

    def sum_mate(o):
        return remote(out_a.at[o], in_a.at[o], sa.at[o], ra.at[o], beside(mate))

    def sum_hi(o, d):
        h = turned(d)
        return remote(out_b.at[o, h], in_b.at[o, hi], sb.at[o, h], rb.at[o, hi], beside(h * 2 + lo))

    def sum_from_hi(o, d):
        h = turned(d)
        return remote(out_b.at[o, h], in_b.at[o, h], sb.at[o, h], rb.at[o, h], beside(h * 2 + lo))

    def to_home(o):
        return remote(out_h.at[o], in_h.at[o], sm.at[o], rm.at[o], ahead(-o))

    fetches[0].wait()
    lanes = lane_index(tokens).astype(jnp.float32)
    routes = [stand_up(route_ref[k:k + 1, :].astype(jnp.float32)) for k in range(2)]
    chosen = ((routes[0] == lanes) | (routes[1] == lanes)).astype(jnp.float32)
    row = lax.broadcasted_iota(jnp.int32, (tokens, tokens), 0)
    column = lax.broadcasted_iota(jnp.int32, (tokens, tokens), 1)
    below = (column <= row).astype(jnp.float32).astype(jnp.bfloat16)
    ranks = dot(below, chosen.astype(jnp.bfloat16))
    slots = lax.broadcasted_iota(jnp.int32, (tokens, CAPACITY), 1).astype(jnp.float32) + 1.0
    tables = []
    for o in range(GROUP):
        here = (ranks[:, o:o + 1] == slots) & (chosen[:, o:o + 1] > 0.5)
        tables.append(here.astype(jnp.float32).astype(jnp.bfloat16))
        table[o] = tables[o]

    def pack(o, k):
        source = x_ref if k == 0 else g_ref
        return dot(tables[o], source[...], TN).astype(jnp.bfloat16)

    for k in range(2):
        fetches[1 + k].wait()
        got[0, me, k] = pack(0, k)
    pl.semaphore_wait(barrier, len(friends))
    for k in range(2):
        for d in range(1, his):
            to_hi(0, k, d).start()
    for o in range(1, GROUP):
        for k in range(2):
            packed[o, k] = pack(o, k)
            to_node(o, k).start()
    for k in range(2):
        to_mate(0, k, hi).start()
    for copy in fetches[3:]:
        copy.wait()

    def spread(o):
        for k in range(2):
            to_node(o, k).wait_recv()
            for d in range(1, his):
                to_hi(o, k, d).start()
            to_mate(o, k, hi).start()

    def pass_on(o):
        for k in range(2):
            for d in range(1, his):
                from_hi(o, k, d).wait_recv()
                to_mate(o, k, turned(d)).start()

    def compute(o):
        for k in range(2):
            for h in range(his):
                from_mate(o, k, h).wait_recv()
        a = b = v = None
        for l in range(locals_):
            rows = pl.ds(l * feat, feat)
            x, g = got[o, l, 0], got[o, l, 1]
            pa, pb, pv = dot(x, gw[rows, :]), dot(x, uw[rows, :]), dot(g, dw[:, rows], NT)
            a, b, v = (pa, pb, pv) if a is None else (a + pa, b + pb, v + pv)
        s = 1.0 / (1.0 + jnp.exp(-a))
        swish = a * s
        part = split_gate(jnp.sum(swish * b * v, axis=1, keepdims=True))
        u = (v * swish).astype(jnp.bfloat16)
        w = (v * b * s * (1.0 + a * (1.0 - s))).astype(jnp.bfloat16)

        def back(l):
            rows = pl.ds(pl.multiple_of(l * feat, 64), feat)
            return dot(w, gw[rows, :], NT) + dot(u, uw[rows, :], NT)

        for h in range(his):
            out_a[o, h, :, pl.ds(0, feat)] = back(h * 2 + 1 - lo).astype(jnp.bfloat16)
            out_a[o, h, :, gate_lanes] = part
        sum_mate(o).start()
        own_gate[...] = part
        for h in range(his):
            own[h] = back(h * 2 + lo)

    def add_mate(o):
        sum_mate(o).wait_recv()
        gate = split_gate(join_gate(own_gate[...]) + join_gate(in_a[o, 0, :, gate_lanes]))
        for d in range(1, his):
            h = turned(d)
            total = own[h] + in_a[o, h, :, pl.ds(0, feat)].astype(jnp.float32)
            out_b[o, h, :, pl.ds(0, feat)] = total.astype(jnp.bfloat16)
            out_b[o, h, :, gate_lanes] = gate
            sum_hi(o, d).start()
        mine[o] = own[hi] + in_a[o, hi, :, pl.ds(0, feat)].astype(jnp.float32)
        in_b[o, hi, :, gate_lanes] = gate

    def add_hi(o):
        total = mine[o]
        for d in range(1, his):
            sum_from_hi(o, d).wait_recv()
            total = total + in_b[o, turned(d), :, pl.ds(0, feat)].astype(jnp.float32)
        gate = join_gate(in_b[o, 0, :, gate_lanes])
        for h in range(1, his):
            gate = gate + join_gate(in_b[o, h, :, gate_lanes])
        out_h[o, :, pl.ds(0, feat)] = total.astype(jnp.bfloat16)
        out_h[o, :, gate_lanes] = split_gate(gate)

        @pl.when(o > 0)
        def _():
            to_home(o).start()

    def step(i, carry):
        @pl.when(i + 1 < GROUP)
        def _():
            spread(i + 1)

        @pl.when(i < GROUP)
        def _():
            pass_on(i)

        @pl.when((i >= 1) & (i <= GROUP))
        def _():
            add_mate(i - 1)

        @pl.when(i >= 2)
        def _():
            add_hi(i - 2)

        @pl.when(i < GROUP)
        def _():
            compute(i)

        return carry

    lax.fori_loop(0, GROUP + 2, step, 0)

    gates = [stand_up(fixed_ref[k:k + 1, :].astype(jnp.float32)) / 65536.0 for k in range(2)]
    total = jnp.zeros((tokens, feat), jnp.float32)
    gate_total = [jnp.zeros((tokens, LANES), jnp.float32) for _ in range(2)]
    for o in range(GROUP):
        if o > 0:
            to_home(o).wait_recv()
        home = out_h if o == 0 else in_h
        hits = [routes[k] == float(o) for k in range(2)]
        weight = sum(jnp.where(hits[k], gates[k], 0.0) for k in range(2))[:, 0:1]
        total = total + weight * dot(table[o], home[o, :, pl.ds(0, feat)])
        back_gate = join_gate(dot(table[o], home[o, :, gate_lanes]))
        for k in range(2):
            gate_total[k] = gate_total[k] + jnp.where(hits[k], back_gate, 0.0)
    out_ref[...] = total.astype(jnp.bfloat16)
    for k in range(2):
        ggrad_ref[k:k + 1, :] = gate_total[k].T[0:1]

    def finish(o, carry):
        for k in range(2):
            for d in range(1, his):
                to_hi(o, k, d).wait_send()
            for h in range(his):
                to_mate(o, k, h).wait_send()
        sum_mate(o).wait_send()
        for d in range(1, his):
            sum_hi(o, d).wait_send()

        @pl.when(o > 0)
        def _():
            for k in range(2):
                to_node(o, k).wait_send()
            to_home(o).wait_send()

        return carry

    lax.fori_loop(0, GROUP, finish, 0)


def body(nodes, locals_, layer_input, output_grad, gate_weight, up_weight, down_weight, route, fixed):
    tokens, feat = layer_input.shape
    width, hidden = gate_weight.shape[1:]
    his = locals_ // 2
    wide = -(-feat // LANES) * LANES + LANES
    bf16, f32 = jnp.bfloat16, jnp.float32
    vmem, dma = pltpu.VMEM, pltpu.SemaphoreType.DMA
    scratch = [
        vmem((tokens, feat), bf16),
        vmem((tokens, feat), bf16),
        vmem((2, tokens), jnp.int32),
        vmem((2, tokens), jnp.int32),
        vmem((width, hidden), bf16),
        vmem((width, hidden), bf16),
        vmem((hidden, width), bf16),
        vmem((GROUP, tokens, CAPACITY), bf16),
        vmem((GROUP, 2, CAPACITY, feat), bf16),
        vmem((GROUP, locals_, 2, CAPACITY, feat), bf16),
        vmem((GROUP, his, CAPACITY, wide), bf16),
        vmem((GROUP, his, CAPACITY, wide), bf16),
        vmem((his, CAPACITY, feat), f32),
        vmem((CAPACITY, LANES), bf16),
        vmem((GROUP, his, CAPACITY, wide), bf16),
        vmem((GROUP, his, CAPACITY, wide), bf16),
        vmem((GROUP, CAPACITY, feat), f32),
        vmem((GROUP, CAPACITY, wide), bf16),
        vmem((GROUP, CAPACITY, wide), bf16),
        dma((7,)),
        dma((GROUP, 2)),
        dma((GROUP, 2)),
        dma((GROUP, 2, his)),
        dma((GROUP, 2, his)),
        dma((GROUP, 2, his)),
        dma((GROUP, 2, his)),
        dma((GROUP,)),
        dma((GROUP,)),
        dma((GROUP, his)),
        dma((GROUP, his)),
        dma((GROUP,)),
        dma((GROUP,)),
    ]
    in_vmem, anywhere = pl.BlockSpec(memory_space=pltpu.VMEM), pl.BlockSpec(memory_space=pl.ANY)
    routed = GROUP * CAPACITY
    grads, gate_grads = pl.pallas_call(
        functools.partial(kernel, nodes, locals_),
        out_shape=(
            jax.ShapeDtypeStruct((tokens, feat), bf16),
            jax.ShapeDtypeStruct((2, tokens), f32),
        ),
        in_specs=[anywhere] * 7,
        out_specs=(in_vmem, in_vmem),
        scratch_shapes=scratch,
        compiler_params=pltpu.CompilerParams(
            collective_id=0, has_side_effects=True, vmem_limit_bytes=60 * 1024 * 1024
        ),
        cost_estimate=pl.CostEstimate(
            flops=10 * routed * width * hidden,
            bytes_accessed=6 * width * hidden + 6 * tokens * feat,
            transcendentals=routed * hidden,
        ),
    )(layer_input, output_grad, gate_weight, up_weight, down_weight, route.T, fixed.T)
    return grads, gate_grads.T


def solution(mesh):
    in_specs = (
        P("node", "local"),
        P("node", "local"),
        P("node", None, "local"),
        P("node", None, "local"),
        P("node", "local", None),
        P("node", None),
        P("node", None),
    )
    out_specs = (P("node", "local"), P("node", None))
    run = functools.partial(body, mesh.shape["node"], mesh.shape["local"])
    return jax.shard_map(run, mesh=mesh, in_specs=in_specs, out_specs=out_specs, check_vma=False)
```

```python
import functools

import jax
import jax.numpy as jnp
from jax import lax
from jax.experimental import pallas as pl
from jax.experimental.pallas import tpu as pltpu
from jax.sharding import PartitionSpec as P

GROUP = 4
CAPACITY = 80
LANES = 128
MESH = pl.DeviceIdType.MESH
NT = (((1,), (1,)), ((), ()))
TN = (((0,), (0,)), ((), ()))


def dot(a, b, dims=None):
    if dims is None:
        return jnp.dot(a, b, preferred_element_type=jnp.float32)
    return lax.dot_general(a, b, dims, preferred_element_type=jnp.float32)


def lane_index(rows):
    return lax.broadcasted_iota(jnp.int32, (rows, LANES), 1)


def split_gate(value):
    high = value.astype(jnp.bfloat16).astype(jnp.float32)
    low = value - high
    return jnp.where(lane_index(value.shape[0]) < LANES // 2, high, low).astype(jnp.bfloat16)


def join_gate(parts):
    lanes = lane_index(parts.shape[0])
    keep = (lanes == 0) | (lanes == LANES // 2)
    return jnp.sum(jnp.where(keep, parts.astype(jnp.float32), 0.0), axis=1, keepdims=True)


def stand_up(row):
    return jnp.broadcast_to(row, (LANES, row.shape[1])).T


def kernel(
    nodes, locals_,
    x_hbm, g_hbm, gate_hbm, up_hbm, down_hbm, route_hbm, fixed_hbm,
    out_ref, ggrad_ref,
    x_ref, g_ref, route_ref, fixed_ref, gw, uw, dw, table, packed, got, out_a, in_a, own, own_gate, out_b, in_b, mine, out_h, in_h,
    wsem, ns, nr, hs, hr, ls, lr, sa, ra, sb, rb, sm, rm,
):
    tokens, feat = x_ref.shape
    wide = out_h.shape[2]
    gate_lanes = pl.ds(wide - LANES, LANES)
    his = locals_ // 2
    node, me = lax.axis_index("node"), lax.axis_index("local")
    hi, lo = me // 2, me % 2
    mate = hi * 2 + (1 - lo)

    def ahead(steps):
        return (lax.rem(node + steps + nodes, nodes), me)

    def beside(index):
        return (node, index)

    def turned(d):
        return lax.rem(hi + d, his)

    fetches = [
        pltpu.make_async_copy(source, dest, wsem.at[i])
        for i, (source, dest) in enumerate((
            (route_hbm, route_ref), (x_hbm, x_ref), (g_hbm, g_ref), (fixed_hbm, fixed_ref),
            (gate_hbm.at[0], gw), (up_hbm.at[0], uw), (down_hbm.at[0], dw),
        ))
    ]
    for copy in fetches:
        copy.start()

    barrier = pltpu.get_barrier_semaphore()
    friends = [ahead(s) for o in range(1, GROUP) for s in (o, -o)]
    friends += [beside(turned(d) * 2 + lo) for d in range(1, his)]
    friends += [beside(mate)]
    for friend in friends:
        pl.semaphore_signal(barrier, inc=1, device_id=friend, device_id_type=MESH)

    def remote(source, dest, send, recv, device):
        return pltpu.make_async_remote_copy(
            src_ref=source, dst_ref=dest, send_sem=send, recv_sem=recv,
            device_id=device, device_id_type=MESH,
        )

    def to_node(o, k):
        return remote(packed.at[o, k], got.at[o, me, k], ns.at[o, k], nr.at[o, k], ahead(o))

    def to_hi(o, k, d):
        return remote(
            got.at[o, me, k], got.at[o, me, k], hs.at[o, k, d], hr.at[o, k, hi],
            beside(turned(d) * 2 + lo),
        )

    def from_hi(o, k, d):
        h = turned(d)
        slot = got.at[o, h * 2 + lo, k]
        return remote(slot, slot, hs.at[o, k, d], hr.at[o, k, h], beside(h * 2 + lo))

    def to_mate(o, k, h):
        slot = got.at[o, h * 2 + lo, k]
        return remote(slot, slot, ls.at[o, k, h], lr.at[o, k, h], beside(mate))

    def from_mate(o, k, h):
        slot = got.at[o, h * 2 + 1 - lo, k]
        return remote(slot, slot, ls.at[o, k, h], lr.at[o, k, h], beside(mate))

    def sum_mate(o):
        return remote(out_a.at[o], in_a.at[o], sa.at[o], ra.at[o], beside(mate))

    def sum_hi(o, d):
        h = turned(d)
        return remote(out_b.at[o, h], in_b.at[o, hi], sb.at[o, h], rb.at[o, hi], beside(h * 2 + lo))

    def sum_from_hi(o, d):
        h = turned(d)
        return remote(out_b.at[o, h], in_b.at[o, h], sb.at[o, h], rb.at[o, h], beside(h * 2 + lo))

    def to_home(o):
        return remote(out_h.at[o], in_h.at[o], sm.at[o], rm.at[o], ahead(-o))

    fetches[0].wait()
    lanes = lane_index(tokens).astype(jnp.float32)
    routes = [stand_up(route_ref[k:k + 1, :].astype(jnp.float32)) for k in range(2)]
    chosen = ((routes[0] == lanes) | (routes[1] == lanes)).astype(jnp.float32)
    row = lax.broadcasted_iota(jnp.int32, (tokens, tokens), 0)
    column = lax.broadcasted_iota(jnp.int32, (tokens, tokens), 1)
    below = (column <= row).astype(jnp.float32).astype(jnp.bfloat16)
    ranks = dot(below, chosen.astype(jnp.bfloat16))
    slots = lax.broadcasted_iota(jnp.int32, (tokens, CAPACITY), 1).astype(jnp.float32) + 1.0
    tables = []
    for o in range(GROUP):
        here = (ranks[:, o:o + 1] == slots) & (chosen[:, o:o + 1] > 0.5)
        tables.append(here.astype(jnp.float32).astype(jnp.bfloat16))
        table[o] = tables[o]

    def pack(o, k):
        source = x_ref if k == 0 else g_ref
        return dot(tables[o], source[...], TN).astype(jnp.bfloat16)

    for k in range(2):
        fetches[1 + k].wait()
        got[0, me, k] = pack(0, k)
    pl.semaphore_wait(barrier, len(friends))
    for k in range(2):
        for d in range(1, his):
            to_hi(0, k, d).start()
    for o in range(1, GROUP):
        for k in range(2):
            packed[o, k] = pack(o, k)
            to_node(o, k).start()
    for k in range(2):
        to_mate(0, k, hi).start()
    for copy in fetches[3:]:
        copy.wait()

    def spread(o):
        for k in range(2):
            to_node(o, k).wait_recv()
            for d in range(1, his):
                to_hi(o, k, d).start()
            to_mate(o, k, hi).start()

    def pass_on(o):
        for k in range(2):
            for d in range(1, his):
                from_hi(o, k, d).wait_recv()
                to_mate(o, k, turned(d)).start()

    def compute(o):
        for k in range(2):
            for h in range(his):
                from_mate(o, k, h).wait_recv()
        a = b = v = None
        for l in range(locals_):
            rows = pl.ds(l * feat, feat)
            x, g = got[o, l, 0], got[o, l, 1]
            pa, pb, pv = dot(x, gw[rows, :]), dot(x, uw[rows, :]), dot(g, dw[:, rows], NT)
            a, b, v = (pa, pb, pv) if a is None else (a + pa, b + pb, v + pv)
        s = 1.0 / (1.0 + jnp.exp(-a))
        swish = a * s
        part = split_gate(jnp.sum(swish * b * v, axis=1, keepdims=True))
        u = (v * swish).astype(jnp.bfloat16)
        w = (v * b * s * (1.0 + a * (1.0 - s))).astype(jnp.bfloat16)

        def back(l):
            rows = pl.ds(pl.multiple_of(l * feat, 64), feat)
            return dot(w, gw[rows, :], NT) + dot(u, uw[rows, :], NT)

        for h in range(his):
            out_a[o, h, :, pl.ds(0, feat)] = back(h * 2 + 1 - lo).astype(jnp.bfloat16)
            out_a[o, h, :, gate_lanes] = part
        sum_mate(o).start()
        own_gate[...] = part
        for h in range(his):
            own[h] = back(h * 2 + lo)

    def add_mate(o):
        sum_mate(o).wait_recv()
        gate = split_gate(join_gate(own_gate[...]) + join_gate(in_a[o, 0, :, gate_lanes]))
        for d in range(1, his):
            h = turned(d)
            total = own[h] + in_a[o, h, :, pl.ds(0, feat)].astype(jnp.float32)
            out_b[o, h, :, pl.ds(0, feat)] = total.astype(jnp.bfloat16)
            out_b[o, h, :, gate_lanes] = gate
            sum_hi(o, d).start()
        mine[o] = own[hi] + in_a[o, hi, :, pl.ds(0, feat)].astype(jnp.float32)
        in_b[o, hi, :, gate_lanes] = gate

    def add_hi(o):
        total = mine[o]
        for d in range(1, his):
            sum_from_hi(o, d).wait_recv()
            total = total + in_b[o, turned(d), :, pl.ds(0, feat)].astype(jnp.float32)
        gate = join_gate(in_b[o, 0, :, gate_lanes])
        for h in range(1, his):
            gate = gate + join_gate(in_b[o, h, :, gate_lanes])
        out_h[o, :, pl.ds(0, feat)] = total.astype(jnp.bfloat16)
        out_h[o, :, gate_lanes] = split_gate(gate)

        @pl.when(o > 0)
        def _():
            to_home(o).start()

    def step(i, carry):
        @pl.when((i >= 1) & (i <= GROUP))
        def _():
            add_mate(i - 1)

        @pl.when(i + 1 < GROUP)
        def _():
            spread(i + 1)

        @pl.when(i < GROUP)
        def _():
            pass_on(i)

        @pl.when(i >= 2)
        def _():
            add_hi(i - 2)

        @pl.when(i < GROUP)
        def _():
            compute(i)

        return carry

    lax.fori_loop(0, GROUP + 2, step, 0)

    gates = [stand_up(fixed_ref[k:k + 1, :].astype(jnp.float32)) / 65536.0 for k in range(2)]
    total = jnp.zeros((tokens, feat), jnp.float32)
    gate_total = [jnp.zeros((tokens, LANES), jnp.float32) for _ in range(2)]
    for o in range(GROUP):
        if o > 0:
            to_home(o).wait_recv()
        home = out_h if o == 0 else in_h
        hits = [routes[k] == float(o) for k in range(2)]
        weight = sum(jnp.where(hits[k], gates[k], 0.0) for k in range(2))[:, 0:1]
        total = total + weight * dot(table[o], home[o, :, pl.ds(0, feat)])
        back_gate = join_gate(dot(table[o], home[o, :, gate_lanes]))
        for k in range(2):
            gate_total[k] = gate_total[k] + jnp.where(hits[k], back_gate, 0.0)
    out_ref[...] = total.astype(jnp.bfloat16)
    for k in range(2):
        ggrad_ref[k:k + 1, :] = gate_total[k].T[0:1]

    def finish(o, carry):
        for k in range(2):
            for d in range(1, his):
                to_hi(o, k, d).wait_send()
            for h in range(his):
                to_mate(o, k, h).wait_send()
        sum_mate(o).wait_send()
        for d in range(1, his):
            sum_hi(o, d).wait_send()

        @pl.when(o > 0)
        def _():
            for k in range(2):
                to_node(o, k).wait_send()
            to_home(o).wait_send()

        return carry

    lax.fori_loop(0, GROUP, finish, 0)


def body(nodes, locals_, layer_input, output_grad, gate_weight, up_weight, down_weight, route, fixed):
    tokens, feat = layer_input.shape
    width, hidden = gate_weight.shape[1:]
    his = locals_ // 2
    wide = -(-feat // LANES) * LANES + LANES
    bf16, f32 = jnp.bfloat16, jnp.float32
    vmem, dma = pltpu.VMEM, pltpu.SemaphoreType.DMA
    scratch = [
        vmem((tokens, feat), bf16),
        vmem((tokens, feat), bf16),
        vmem((2, tokens), jnp.int32),
        vmem((2, tokens), jnp.int32),
        vmem((width, hidden), bf16),
        vmem((width, hidden), bf16),
        vmem((hidden, width), bf16),
        vmem((GROUP, tokens, CAPACITY), bf16),
        vmem((GROUP, 2, CAPACITY, feat), bf16),
        vmem((GROUP, locals_, 2, CAPACITY, feat), bf16),
        vmem((GROUP, his, CAPACITY, wide), bf16),
        vmem((GROUP, his, CAPACITY, wide), bf16),
        vmem((his, CAPACITY, feat), f32),
        vmem((CAPACITY, LANES), bf16),
        vmem((GROUP, his, CAPACITY, wide), bf16),
        vmem((GROUP, his, CAPACITY, wide), bf16),
        vmem((GROUP, CAPACITY, feat), f32),
        vmem((GROUP, CAPACITY, wide), bf16),
        vmem((GROUP, CAPACITY, wide), bf16),
        dma((7,)),
        dma((GROUP, 2)),
        dma((GROUP, 2)),
        dma((GROUP, 2, his)),
        dma((GROUP, 2, his)),
        dma((GROUP, 2, his)),
        dma((GROUP, 2, his)),
        dma((GROUP,)),
        dma((GROUP,)),
        dma((GROUP, his)),
        dma((GROUP, his)),
        dma((GROUP,)),
        dma((GROUP,)),
    ]
    in_vmem, anywhere = pl.BlockSpec(memory_space=pltpu.VMEM), pl.BlockSpec(memory_space=pl.ANY)
    routed = GROUP * CAPACITY
    grads, gate_grads = pl.pallas_call(
        functools.partial(kernel, nodes, locals_),
        out_shape=(
            jax.ShapeDtypeStruct((tokens, feat), bf16),
            jax.ShapeDtypeStruct((2, tokens), f32),
        ),
        in_specs=[anywhere] * 7,
        out_specs=(in_vmem, in_vmem),
        scratch_shapes=scratch,
        compiler_params=pltpu.CompilerParams(
            collective_id=0, has_side_effects=True, vmem_limit_bytes=60 * 1024 * 1024
        ),
        cost_estimate=pl.CostEstimate(
            flops=10 * routed * width * hidden,
            bytes_accessed=6 * width * hidden + 6 * tokens * feat,
            transcendentals=routed * hidden,
        ),
    )(layer_input, output_grad, gate_weight, up_weight, down_weight, route.T, fixed.T)
    return grads, gate_grads.T


def solution(mesh):
    in_specs = (
        P("node", "local"),
        P("node", "local"),
        P("node", None, "local"),
        P("node", None, "local"),
        P("node", "local", None),
        P("node", None),
        P("node", None),
    )
    out_specs = (P("node", "local"), P("node", None))
    run = functools.partial(body, mesh.shape["node"], mesh.shape["local"])
    return jax.shard_map(run, mesh=mesh, in_specs=in_specs, out_specs=out_specs, check_vma=False)
```
